256 devices in a mesh: orb: 64 (over z, x, core), rep: 4 (over y).
Axes of the slice: x: 4, y: 4, z: 8, core: 2. Of those that a mesh axis runs over, the one named last changes fastest.
Arguments:
- observed: float32 [512, 256], P('orb'), may hold values from -6 to 6
- weights: float32 [512, 256], P('orb'), may hold values from 0.25 to 4
- precision_prior: float32 [2048, 1024], P('orb', 'rep'), may hold values from 0.5 to 4
- footprint: bfloat16 [3072, 256, 1024], P('orb', None, 'rep'), may hold values from -0.1875 to 0.1875
- block_rows: int32 [3072], P('orb'), may hold values from 0 to 511, as said below
- block_cells: int32 [3072], P('orb'), may hold values from 0 to 2047, as said below
Outputs:
- solution: float32 [2048, 1024], P('orb', 'rep')
- residual: float32 [2048, 1024], P('orb', 'rep')
The draws below stay inside these ranges and needn't reach their ends.
Inputs may be any that keep to these rules, and one draw needn't show every extreme that they name: `block_rows`: the listed blocks of orbit group g (rows g * 48 to (g + 1) * 48 - 1) name only sounding blocks g * 8 to (g + 1) * 8 - 1. `block_cells`: region group r holds cell-period blocks r * 32 to (r + 1) * 32 - 1. The first 2 listed blocks of every orbit group name cell-period blocks of one common region group; no orbit group names cell-period blocks of one region group in more than 2 of its listed blocks.
All inputs are finite; a program needn't handle non-finite values.
Results may differ from the reference program's by a relative error of at most 0.0015.
Values sent between devices are 32-bit elements; how exact they have to be, the bound alone decides.
No kernel may reach another device: no remote copies, remote signals or barrier semaphores. Data moves between devices by JAX's collectives and lax.ppermute only.
A program may use at most 64 MiB of HBM per device.

```python
import math
import jax
import jax.numpy as jnp
from jax import lax

SBS = 256
CBS = 1024
SB_DEV = 8
NB_DEV = 48
CB_DEV = 32
ITERS = 4
CAP = 2
NSB = 512
NCB = 2048
NBLK = 3072
N_ORB = 64


def draw_block_rows(key, part):
    key = jax.random.fold_in(key, 5)
    local_ids = jax.random.randint(key, (N_ORB, NB_DEV), 0, SB_DEV)
    group_ids = jnp.arange(N_ORB, dtype=jnp.int32)[:, None]
    return (group_ids * SB_DEV + local_ids).reshape(-1).astype(jnp.int32)


def draw_block_cells(key, part):
    key = jax.random.fold_in(key, 11)
    key_hot, key_start, key_slot = jax.random.split(key, 3)
    hottest = jax.random.randint(key_hot, (), 0, N_ORB)
    starts = jax.random.randint(key_start, (N_ORB, 1), 0, N_ORB - 1)
    counter = jnp.arange(NB_DEV, dtype=jnp.int32)[None, :]
    others = (hottest + 1 + (starts + counter - CAP) % (N_ORB - 1)) % N_ORB
    owners = jnp.where(counter < CAP, hottest, others)
    slot_ids = jax.random.randint(key_slot, (N_ORB, NB_DEV), 0, CB_DEV)
    return (owners * CB_DEV + slot_ids).reshape(-1).astype(jnp.int32)


def shard_levels(rng, shape, cuts, least, top_value):
    level, own = 1.0, jax.random.fold_in(rng, 6)
    for axis_at, blocks in cuts:
        draws = jnp.exp(jax.random.uniform(jax.random.fold_in(own, axis_at), (blocks,), jnp.float32, least / len(cuts), top_value / len(cuts)))
        level = level * jnp.repeat(draws, shape[axis_at] // blocks).reshape([-1 if axis == axis_at else 1 for axis in range(len(shape))])
    return level


def gaussian(key, dims, scale, bound, cuts=(), kind=jnp.bfloat16):
    drawn = jax.random.normal(key, dims, jnp.float32) * scale
    if len(cuts) > 0:
        drawn = shard_levels(key, dims, cuts, -0.22, 0.18) * drawn
    return jnp.clip(drawn, min=-bound, max=bound).astype(kind)


def setup_inputs(seed: int = 0) -> dict:
    streams_of = jax.random.split(jax.random.key(seed), 7)
    observed = gaussian(streams_of[0], (NSB, SBS), 1.0, 6.0, ((0, 64),), jnp.float32)
    weights = jnp.clip(jnp.exp(math.log(4.0) - 2.7725887 * jax.random.uniform(streams_of[1], (NSB, SBS), jnp.float32) ** shard_levels(streams_of[1], (NSB, SBS), ((0, 64),), -0.2, 0.2)), 0.25, 4.0)
    precision_prior = jnp.clip(jnp.exp(math.log(4.0) - 2.0794415 * jax.random.uniform(streams_of[2], (NCB, CBS), jnp.float32) ** shard_levels(streams_of[2], (NCB, CBS), ((0, 64), (1, 4)), -0.2, 0.2)), 0.5, 4.0)
    footprint = gaussian(streams_of[3], (NBLK, SBS, CBS), CBS ** -0.5, 0.1875, ((0, 64), (2, 4)))
    block_rows = draw_block_rows(jax.random.fold_in(streams_of[6], 71), 0)
    block_cells = draw_block_cells(jax.random.fold_in(streams_of[6], 71), 0)
    return dict(observed=observed, weights=weights, precision_prior=precision_prior, footprint=footprint, block_rows=block_rows, block_cells=block_cells)


def forward(footprint, block_rows, block_cells, flux):
    groups = footprint.reshape(N_ORB, NB_DEV, SBS, CBS)
    cell_ids = block_cells.reshape(N_ORB, NB_DEV)

    def single(member):
        blocks, chosen = member
        return jnp.einsum("bsc,bc->bs", blocks.astype(jnp.float32), flux[chosen], precision=lax.Precision.HIGHEST)

    results = lax.map(single, (groups, cell_ids))
    return jax.ops.segment_sum(results.reshape(NBLK, SBS), block_rows, num_segments=NSB)


def adjoint(footprint, block_rows, block_cells, field):
    groups = footprint.reshape(N_ORB, NB_DEV, SBS, CBS)
    row_ids = block_rows.reshape(N_ORB, NB_DEV)

    def single(member):
        blocks, chosen = member
        return jnp.einsum("bsc,bs->bc", blocks.astype(jnp.float32), field[chosen], precision=lax.Precision.HIGHEST)

    results = lax.map(single, (groups, row_ids))
    return jax.ops.segment_sum(results.reshape(NBLK, CBS), block_cells, num_segments=NCB)


def reference(observed, weights, precision_prior, footprint, block_rows, block_cells):
    gradient = adjoint(footprint, block_rows, block_cells, weights * observed)
    solution = jnp.zeros_like(gradient)
    residual = gradient
    direction = gradient
    norm_now = jnp.sum(residual * residual)
    for iteration in range(ITERS):
        image = adjoint(footprint, block_rows, block_cells, weights * forward(footprint, block_rows, block_cells, direction))
        image = image + precision_prior * direction
        alpha = norm_now / jnp.sum(direction * image)
        solution = solution + alpha * direction
        residual = residual - alpha * image
        norm_next = jnp.sum(residual * residual)
        direction = residual + (norm_next / norm_now) * direction
        norm_now = norm_next
    return solution, residual
```

```python
import functools

import jax
import jax.numpy as jnp
from jax import lax
from jax.experimental import pallas as pl
from jax.experimental.pallas import tpu as pltpu
from jax.sharding import PartitionSpec as P

ITERS = 4
CAP = 2
LANES = 128
MSG = 2 * CAP + 1
SUB = 16
F32 = jnp.float32
BF16 = jnp.bfloat16


def lane_ids(shape):
    return lax.broadcasted_iota(jnp.int32, shape, len(shape) - 1)


def three_parts(values):
    high = values.astype(BF16)
    rest = values - high.astype(F32)
    middle = rest.astype(BF16)
    low = (rest - middle.astype(F32)).astype(BF16)
    return high, middle, low


def spread(packed, field_ref):
    rows, soundings, _ = field_ref.shape
    for group in range(soundings // 8):
        for row in range(rows):
            lane = rows * group + row
            field_ref[row, 8 * group : 8 * group + 8, :] = jnp.broadcast_to(
                packed[:, lane : lane + 1], (8, LANES)
            )


def transposed_products(footprint_ref, field_ref, out_ref, blocks, row_of, place_of):
    soundings = footprint_ref.shape[1]

    def body(block, carry):
        row = row_of(block)
        place = place_of(block)
        left = jnp.zeros((SUB, LANES), F32)
        right = jnp.zeros((SUB, LANES), F32)
        for start in range(0, soundings, SUB):
            part = footprint_ref[block, start : start + SUB, :].astype(F32)
            z = field_ref[row, start : start + SUB, :]
            left = left + part[:, :LANES] * z
            right = right + part[:, LANES:] * z
        out_ref[pl.ds(place, 1), :] = jnp.sum(left, axis=0, keepdims=True)
        out_ref[pl.ds(place + 1, 1), :] = jnp.sum(right, axis=0, keepdims=True)
        return carry

    lax.fori_loop(0, blocks, body, 0)


def start_kernel(rows_ref, cells_ref, packed_ref, footprint_ref, out_ref, meta_ref, field_ref, count_ref):
    blocks = rows_ref.shape[0]
    rows = field_ref.shape[0]
    orbits = out_ref.shape[0] // MSG
    cells = 32
    out_ref[...] = jnp.zeros_like(out_ref)
    spread(packed_ref[...], field_ref)

    def clear(owner, carry):
        count_ref[owner] = 0
        return carry

    lax.fori_loop(0, orbits, clear, 0)

    def place_block(block, carry):
        cell = cells_ref[block]
        owner = cell // cells
        slot = cell % cells
        rank = count_ref[owner]
        count_ref[owner] = rank + 1
        meta_ref[block] = owner * MSG + 2 * rank
        meta_ref[blocks + block] = rows_ref[block] % rows
        scalars = pl.ds(owner * MSG + 2 * CAP, 1)
        out_ref[scalars, :] = jnp.where(
            lane_ids((1, LANES)) == rank, (slot + 1).astype(F32), out_ref[scalars, :]
        )
        return carry

    lax.fori_loop(0, blocks, place_block, 0)
    transposed_products(
        footprint_ref, field_ref, out_ref, blocks, lambda b: meta_ref[blocks + b], lambda b: meta_ref[b]
    )


def serve(residual, pick, scalars, out_ref):
    orbits = out_ref.shape[0] // MSG
    high, middle, low = three_parts(residual)
    stacked = jnp.concatenate([high, middle, low, jnp.zeros_like(high)], axis=0)
    pieces = jnp.dot(pick, stacked, preferred_element_type=F32)
    for slot in range(CAP):
        for half in range(2):
            out_ref[pl.ds(2 * slot + half, orbits, stride=MSG), :] = pieces[
                slot * orbits : (slot + 1) * orbits, half * LANES : (half + 1) * LANES
            ]
    out_ref[pl.ds(2 * CAP, orbits, stride=MSG), :] = jnp.broadcast_to(scalars, (orbits, LANES))


def gathered(in_ref, collect):
    orbits = in_ref.shape[0] // MSG
    slots = [
        jnp.concatenate(
            [in_ref[pl.ds(2 * slot + half, orbits, stride=MSG), :] for half in range(2)], axis=1
        )
        for slot in range(CAP)
    ]
    high, middle, low = three_parts(jnp.concatenate(slots, axis=0))
    return jnp.dot(collect, jnp.concatenate([high, middle, low], axis=0), preferred_element_type=F32)


def row_of_scalars(values):
    lanes = lane_ids((1, LANES))
    row = jnp.zeros((1, LANES), F32)
    for lane, value in enumerate(values):
        row = jnp.where(lanes == lane, value, row)
    return row


def total(values):
    return jnp.sum(jnp.sum(values, axis=0, keepdims=True), axis=1, keepdims=True)


def first_owner_kernel(in_ref, prior_ref, residual_ref, out_ref, collect_ref, pick_ref):
    orbits = in_ref.shape[0] // MSG
    cells = prior_ref.shape[0]
    ids = in_ref[pl.ds(2 * CAP, orbits, stride=MSG), :]
    lanes = lane_ids((orbits, LANES)).astype(F32)
    pick = jnp.concatenate(
        [(ids[:, slot : slot + 1] == lanes + 1.0).astype(F32) for slot in range(CAP)], axis=0
    )
    pick = jnp.where(lane_ids(pick.shape) < cells, pick, 0.0)
    collect = pick.T[:cells, :]
    collect_ref[...] = jnp.concatenate([collect] * 3, axis=1).astype(BF16)
    folds = [pick[:, :cells]] * 3 + [jnp.zeros((pick.shape[0], LANES - 3 * cells), F32)]
    pick_ref[...] = jnp.concatenate(folds, axis=1).astype(BF16)
    residual = gathered(in_ref, collect_ref[...])
    residual_ref[...] = residual
    squares = residual * residual
    scalars = row_of_scalars([total(squares), total(prior_ref[...] * squares)])
    serve(residual, pick_ref[...], scalars, out_ref)


def owner_kernel(
    last, first, in_ref, scalars_ref, prior_ref, collect_ref, pick_ref, residual_ref, direction_ref,
    solution_ref, new_residual_ref, new_solution_ref, new_direction_ref=None, out_ref=None
):
    orbits = in_ref.shape[0] // MSG
    prior = prior_ref[...]
    norm = scalars_ref[0:1, 0:1]
    weighted = scalars_ref[0:1, 1:2]
    beta = scalars_ref[0:1, 2:3]
    forward = jnp.sum(in_ref[pl.ds(2 * CAP, orbits, stride=MSG), :], axis=0, keepdims=True)[:, 0:1]
    alpha = norm / (forward + weighted)
    residual = residual_ref[...]
    direction = residual if first else residual + beta * direction_ref[...]
    image = gathered(in_ref, collect_ref[...]) + prior * direction
    solution = alpha * direction if first else solution_ref[...] + alpha * direction
    residual = residual - alpha * image
    new_residual_ref[...] = residual
    new_solution_ref[...] = solution
    if not last:
        new_direction_ref[...] = direction
        scaled = prior * residual
        scalars = row_of_scalars(
            [total(residual * residual), total(scaled * residual), total(scaled * direction)]
        )
        serve(residual, pick_ref[...], scalars, out_ref)


def forward_kernel(meta_ref, in_ref, footprint_ref, out_ref, sums_ref):
    blocks = footprint_ref.shape[0]
    rows, soundings, _ = sums_ref.shape
    orbits = in_ref.shape[0] // MSG
    sums_ref[...] = jnp.zeros_like(sums_ref)

    def body(block, carry):
        place = meta_ref[block]
        row = meta_ref[blocks + block]
        left = jnp.broadcast_to(in_ref[pl.ds(place, 1), :], (SUB, LANES))
        right = jnp.broadcast_to(in_ref[pl.ds(place + 1, 1), :], (SUB, LANES))
        for start in range(0, soundings, SUB):
            part = footprint_ref[block, start : start + SUB, :].astype(F32)
            sums_ref[row, start : start + SUB, :] += part[:, :LANES] * left + part[:, LANES:] * right
        return carry

    lax.fori_loop(0, blocks, body, 0)
    lanes = lane_ids((8, LANES))
    per_half = LANES // rows
    halves = []
    for half in range(soundings // 8 // per_half):
        packed = jnp.zeros((8, LANES), F32)
        for at in range(per_half):
            group = half * per_half + at
            for row in range(rows):
                summed = jnp.sum(sums_ref[row, 8 * group : 8 * group + 8, :], axis=1, keepdims=True)
                packed = jnp.where(lanes == rows * at + row, summed, packed)
        halves.append(packed)
    scalars = jnp.sum(in_ref[pl.ds(2 * CAP, orbits, stride=MSG), :], axis=0, keepdims=True)
    halves.append(jnp.broadcast_to(scalars, (8, LANES)))
    message = jnp.concatenate(halves, axis=0)
    for peer in range(out_ref.shape[0]):
        out_ref[peer] = message


def adjoint_kernel(
    first, meta_ref, in_ref, weights_ref, footprint_ref, image_ref, scalars_ref,
    out_ref, new_image_ref, new_scalars_ref, field_ref
):
    blocks = footprint_ref.shape[0]
    orbits = out_ref.shape[0] // MSG
    summed = in_ref[0]
    for peer in range(1, in_ref.shape[0]):
        summed = summed + in_ref[peer]
    forward = jnp.concatenate([summed[0:8], summed[8:16]], axis=1)
    norm = summed[16:17, 0:1]
    weighted = summed[16:17, 1:2]
    beta = jnp.zeros((1, 1), F32)
    if not first:
        beta = norm / scalars_ref[0:1, 0:1]
        cross = summed[16:17, 2:3]
        weighted = weighted + 2.0 * beta * cross + beta * beta * scalars_ref[0:1, 1:2]
        forward = forward + beta * image_ref[...]
    new_image_ref[...] = forward
    new_scalars_ref[...] = jnp.broadcast_to(row_of_scalars([norm, weighted, beta]), (8, LANES))
    field = weights_ref[...] * forward
    out_ref[...] = jnp.zeros_like(out_ref)
    out_ref[pl.ds(2 * CAP, orbits, stride=MSG), :] = jnp.broadcast_to(
        row_of_scalars([total(field * forward)]), (orbits, LANES)
    )
    spread(field, field_ref)
    transposed_products(
        footprint_ref, field_ref, out_ref, blocks, lambda b: meta_ref[blocks + b], lambda b: meta_ref[b]
    )


def call(kernel, out_shape, kinds, out_kinds=None, scratch=()):
    spaces = {"v": pltpu.VMEM, "s": pltpu.SMEM}
    single = not isinstance(out_shape, (list, tuple))
    out_kinds = out_kinds or "v" * (1 if single else len(out_shape))
    out_specs = [pl.BlockSpec(memory_space=spaces[kind]) for kind in out_kinds]
    return pl.pallas_call(
        kernel,
        out_shape=out_shape,
        in_specs=[pl.BlockSpec(memory_space=spaces[kind]) for kind in kinds],
        out_specs=out_specs[0] if single else out_specs,
        scratch_shapes=list(scratch),
        compiler_params=pltpu.CompilerParams(vmem_limit_bytes=32 * 1024 * 1024),
    )


def per_device(observed, weights, precision_prior, footprint, block_rows, block_cells):
    rows, soundings = observed.shape
    cells, width = precision_prior.shape
    blocks = footprint.shape[0]
    orbits = lax.axis_size("orb")
    reps = lax.axis_size("rep")
    shape = jax.ShapeDtypeStruct
    messages = shape((orbits * MSG, LANES), F32)
    packed_shape = shape((8, soundings * rows // 8), F32)
    scalar_shape = shape((8, LANES), F32)
    region = shape((cells, width), F32)
    field = pltpu.VMEM((rows, soundings, LANES), F32)

    def pack(values):
        return values.reshape(rows, soundings // 8, 8).transpose(2, 1, 0).reshape(packed_shape.shape)

    def exchange(array):
        array = array.reshape(orbits, 1, MSG * LANES)
        array = lax.all_to_all(array, "orb", split_axis=0, concat_axis=0, tiled=True)
        return array.reshape(messages.shape)

    footprint = pltpu.with_memory_space_constraint(footprint, pltpu.VMEM)
    packed_weights = pack(weights)
    outgoing, meta = call(
        start_kernel,
        [messages, shape((2 * blocks,), jnp.int32)],
        "ssvv",
        "vs",
        [field, pltpu.SMEM((orbits,), jnp.int32)],
    )(block_rows, block_cells, pack(weights * observed), footprint)
    incoming = exchange(outgoing)
    residual, outgoing, collect, pick = call(
        first_owner_kernel,
        [
            region,
            messages,
            shape((cells, 3 * CAP * orbits), BF16),
            shape((CAP * orbits, LANES), BF16),
        ],
        "vv",
    )(incoming, precision_prior)
    direction = solution = residual
    image = jnp.zeros(packed_shape.shape, F32)
    scalars = jnp.zeros(scalar_shape.shape, F32)
    for iteration in range(ITERS):
        first, last = iteration == 0, iteration == ITERS - 1
        partial = call(
            forward_kernel,
            shape((reps, 24, LANES), F32),
            "svv",
            scratch=[field],
        )(meta, exchange(outgoing), footprint)
        partial = lax.all_to_all(partial, "rep", split_axis=0, concat_axis=0, tiled=True)
        outgoing, image, scalars = call(
            functools.partial(adjoint_kernel, first),
            [messages, packed_shape, scalar_shape],
            "svvvvv",
            scratch=[field],
        )(meta, partial, packed_weights, footprint, image, scalars)
        incoming = exchange(outgoing)
        results = call(
            functools.partial(owner_kernel, last, first),
            [region, region] if last else [region, region, region, messages],
            "vvvvvvvv",
        )(incoming, scalars, precision_prior, collect, pick, residual, direction, solution)
        residual, solution = results[:2]
        if not last:
            direction, outgoing = results[2:]
    return (solution, residual)


def solution(mesh):
    in_specs = (
        P("orb", None),
        P("orb", None),
        P("orb", "rep"),
        P("orb", None, "rep"),
        P("orb"),
        P("orb"),
    )
    out_specs = (P("orb", "rep"), P("orb", "rep"))
    return jax.shard_map(
        per_device, mesh=mesh, in_specs=in_specs, out_specs=out_specs, check_vma=False
    )
```

```python
import functools

import jax
import jax.numpy as jnp
from jax import lax
from jax.experimental import pallas as pl
from jax.experimental.pallas import tpu as pltpu
from jax.sharding import PartitionSpec as P

ITERS = 4
CAP = 2
LANES = 128
MSG = 2 * CAP + 1
SUB = 16
F32 = jnp.float32
BF16 = jnp.bfloat16


def lane_ids(shape):
    return lax.broadcasted_iota(jnp.int32, shape, len(shape) - 1)


def three_parts(values):
    high = values.astype(BF16)
    rest = values - high.astype(F32)
    middle = rest.astype(BF16)
    low = (rest - middle.astype(F32)).astype(BF16)
    return high, middle, low


def spread(packed, field_ref):
    rows, soundings, _ = field_ref.shape
    for group in range(soundings // 8):
        for row in range(rows):
            lane = rows * group + row
            field_ref[row, 8 * group : 8 * group + 8, :] = jnp.broadcast_to(
                packed[:, lane : lane + 1], (8, LANES)
            )


def transposed_products(footprint_ref, field_ref, out_ref, meta_ref, first, last, together=4):
    soundings = footprint_ref.shape[1]
    blocks = footprint_ref.shape[0]

    def product(block):
        row = meta_ref[blocks + block]
        place = meta_ref[block]
        left = jnp.zeros((SUB, LANES), F32)
        right = jnp.zeros((SUB, LANES), F32)
        for start in range(0, soundings, SUB):
            part = footprint_ref[block, start : start + SUB, :].astype(F32)
            z = field_ref[row, start : start + SUB, :]
            left = left + part[:, :LANES] * z
            right = right + part[:, LANES:] * z
        out_ref[pl.ds(place, 1), :] = jnp.sum(left, axis=0, keepdims=True)
        out_ref[pl.ds(place + 1, 1), :] = jnp.sum(right, axis=0, keepdims=True)

    def body(step, carry):
        for at in range(together):
            product(first + step * together + at)
        return carry

    lax.fori_loop(0, (last - first) // together, body, 0)


def in_columns(values):
    rows, soundings = values.shape
    parts = []
    for start in range(0, soundings, LANES):
        part = values[:, start : start + LANES]
        parts.append(jnp.concatenate([part] * (LANES // rows), axis=0).T)
    return jnp.concatenate(parts, axis=0)


def start_kernel(
    cells, rows_hbm, cells_hbm, observed_hbm, weights_hbm, footprint_hbm,
    out_ref, meta_ref, packed_ref, footprint_ref,
    field_ref, count_ref, rows_ref, cells_ref, observed_ref, weights_ref, sems, chunk_sems
):
    blocks = footprint_ref.shape[0]
    rows, soundings = weights_ref.shape
    orbits = out_ref.shape[0] // MSG
    chunks = chunk_sems.shape[0]
    size = blocks // chunks
    small = [
        pltpu.make_async_copy(source, target, sems.at[at])
        for at, (source, target) in enumerate(
            [
                (rows_hbm, rows_ref),
                (cells_hbm, cells_ref),
                (observed_hbm, observed_ref),
                (weights_hbm, weights_ref),
            ]
        )
    ]
    for copy in small:
        copy.start()
    large = []
    for chunk in range(chunks):
        span = pl.ds(chunk * size, size)
        large.append(
            pltpu.make_async_copy(footprint_hbm.at[span], footprint_ref.at[span], chunk_sems.at[chunk])
        )
        large[-1].start()
    out_ref[...] = jnp.zeros_like(out_ref)
    for owner in range(orbits):
        count_ref[owner] = 0
    for copy in small:
        copy.wait()
    weights = weights_ref[...]
    columns = in_columns(weights * observed_ref[...])
    for row in range(rows):
        field_ref[row] = jnp.broadcast_to(columns[:, row : row + 1], (soundings, LANES))
    columns = in_columns(weights)
    groups = LANES // rows
    lanes = lane_ids((8, LANES)) // rows
    for half in range(soundings // LANES):
        packed = jnp.zeros((8, LANES), F32)
        for at in range(groups):
            start = half * LANES + 8 * at
            packed = jnp.where(lanes == at, columns[start : start + 8, :], packed)
        packed_ref[:, half * LANES : (half + 1) * LANES] = packed

    def place_block(block, carry):
        cell = cells_ref[block]
        owner = cell // cells
        slot = cell % cells
        rank = count_ref[owner]
        count_ref[owner] = rank + 1
        meta_ref[block] = owner * MSG + 2 * rank
        meta_ref[blocks + block] = rows_ref[block] % rows
        scalars = pl.ds(owner * MSG + 2 * CAP, 1)
        out_ref[scalars, :] = jnp.where(
            lane_ids((1, LANES)) == rank, (slot + 1).astype(F32), out_ref[scalars, :]
        )
        return carry

    lax.fori_loop(0, blocks, place_block, 0)
    for chunk in range(chunks):
        large[chunk].wait()
        transposed_products(
            footprint_ref, field_ref, out_ref, meta_ref, chunk * size, (chunk + 1) * size
        )


def serve(residual, pick, scalars, out_ref):
    orbits = out_ref.shape[0] // MSG
    high, middle, low = three_parts(residual)
    stacked = jnp.concatenate([high, middle, low, jnp.zeros_like(high)], axis=0)
    pieces = jnp.dot(pick, stacked, preferred_element_type=F32)
    for slot in range(CAP):
        for half in range(2):
            out_ref[pl.ds(2 * slot + half, orbits, stride=MSG), :] = pieces[
                slot * orbits : (slot + 1) * orbits, half * LANES : (half + 1) * LANES
            ]
    out_ref[pl.ds(2 * CAP, orbits, stride=MSG), :] = jnp.broadcast_to(scalars, (orbits, LANES))


def gathered(in_ref, collect):
    orbits = in_ref.shape[0] // MSG
    slots = [
        jnp.concatenate(
            [in_ref[pl.ds(2 * slot + half, orbits, stride=MSG), :] for half in range(2)], axis=1
        )
        for slot in range(CAP)
    ]
    high, middle, low = three_parts(jnp.concatenate(slots, axis=0))
    return jnp.dot(collect, jnp.concatenate([high, middle, low], axis=0), preferred_element_type=F32)


def row_of_scalars(values):
    lanes = lane_ids((1, LANES))
    row = jnp.zeros((1, LANES), F32)
    for lane, value in enumerate(values):
        row = jnp.where(lanes == lane, value, row)
    return row


def total(values):
    return jnp.sum(jnp.sum(values, axis=0, keepdims=True), axis=1, keepdims=True)


def first_owner_kernel(in_ref, prior_ref, residual_ref, out_ref, collect_ref, pick_ref):
    orbits = in_ref.shape[0] // MSG
    cells = prior_ref.shape[0]
    ids = in_ref[pl.ds(2 * CAP, orbits, stride=MSG), :]
    lanes = lane_ids((orbits, LANES)).astype(F32)
    pick = jnp.concatenate(
        [(ids[:, slot : slot + 1] == lanes + 1.0).astype(F32) for slot in range(CAP)], axis=0
    )
    pick = jnp.where(lane_ids(pick.shape) < cells, pick, 0.0)
    collect = pick.T[:cells, :]
    collect_ref[...] = jnp.concatenate([collect] * 3, axis=1).astype(BF16)
    folds = [pick[:, :cells]] * 3 + [jnp.zeros((pick.shape[0], LANES - 3 * cells), F32)]
    pick_ref[...] = jnp.concatenate(folds, axis=1).astype(BF16)
    residual = gathered(in_ref, collect_ref[...])
    residual_ref[...] = residual
    squares = residual * residual
    scalars = row_of_scalars([total(squares), total(prior_ref[...] * squares)])
    serve(residual, pick_ref[...], scalars, out_ref)


def owner_kernel(
    last, first, in_ref, scalars_ref, prior_ref, collect_ref, pick_ref, residual_ref, direction_ref,
    solution_ref, new_residual_ref, new_solution_ref, new_direction_ref=None, out_ref=None
):
    orbits = in_ref.shape[0] // MSG
    prior = prior_ref[...]
    norm = scalars_ref[0:1, 0:1]
    weighted = scalars_ref[0:1, 1:2]
    beta = scalars_ref[0:1, 2:3]
    forward = jnp.sum(in_ref[pl.ds(2 * CAP, orbits, stride=MSG), :], axis=0, keepdims=True)[:, 0:1]
    alpha = norm / (forward + weighted)
    residual = residual_ref[...]
    direction = residual if first else residual + beta * direction_ref[...]
    image = gathered(in_ref, collect_ref[...]) + prior * direction
    solution = alpha * direction if first else solution_ref[...] + alpha * direction
    residual = residual - alpha * image
    new_residual_ref[...] = residual
    new_solution_ref[...] = solution
    if not last:
        new_direction_ref[...] = direction
        scaled = prior * residual
        scalars = row_of_scalars(
            [total(residual * residual), total(scaled * residual), total(scaled * direction)]
        )
        serve(residual, pick_ref[...], scalars, out_ref)


def forward_kernel(meta_ref, in_ref, footprint_ref, out_ref, sums_ref):
    blocks = footprint_ref.shape[0]
    rows, soundings, _ = sums_ref.shape
    orbits = in_ref.shape[0] // MSG
    sums_ref[...] = jnp.zeros_like(sums_ref)

    def body(block, carry):
        place = meta_ref[block]
        row = meta_ref[blocks + block]
        left = jnp.broadcast_to(in_ref[pl.ds(place, 1), :], (SUB, LANES))
        right = jnp.broadcast_to(in_ref[pl.ds(place + 1, 1), :], (SUB, LANES))
        for start in range(0, soundings, SUB):
            part = footprint_ref[block, start : start + SUB, :].astype(F32)
            sums_ref[row, start : start + SUB, :] += part[:, :LANES] * left + part[:, LANES:] * right
        return carry

    lax.fori_loop(0, blocks, body, 0)
    lanes = lane_ids((8, LANES))
    per_half = LANES // rows
    halves = []
    for half in range(soundings // 8 // per_half):
        packed = jnp.zeros((8, LANES), F32)
        for at in range(per_half):
            group = half * per_half + at
            for row in range(rows):
                summed = jnp.sum(sums_ref[row, 8 * group : 8 * group + 8, :], axis=1, keepdims=True)
                packed = jnp.where(lanes == rows * at + row, summed, packed)
        halves.append(packed)
    scalars = jnp.sum(in_ref[pl.ds(2 * CAP, orbits, stride=MSG), :], axis=0, keepdims=True)
    halves.append(jnp.broadcast_to(scalars, (8, LANES)))
    message = jnp.concatenate(halves, axis=0)
    for peer in range(out_ref.shape[0]):
        out_ref[peer] = message


def adjoint_kernel(
    first, meta_ref, in_ref, weights_ref, footprint_ref, image_ref, scalars_ref,
    out_ref, new_image_ref, new_scalars_ref, field_ref
):
    orbits = out_ref.shape[0] // MSG
    summed = in_ref[0]
    for peer in range(1, in_ref.shape[0]):
        summed = summed + in_ref[peer]
    forward = jnp.concatenate([summed[0:8], summed[8:16]], axis=1)
    norm = summed[16:17, 0:1]
    weighted = summed[16:17, 1:2]
    beta = jnp.zeros((1, 1), F32)
    if not first:
        beta = norm / scalars_ref[0:1, 0:1]
        cross = summed[16:17, 2:3]
        weighted = weighted + 2.0 * beta * cross + beta * beta * scalars_ref[0:1, 1:2]
        forward = forward + beta * image_ref[...]
    new_image_ref[...] = forward
    new_scalars_ref[...] = jnp.broadcast_to(row_of_scalars([norm, weighted, beta]), (8, LANES))
    field = weights_ref[...] * forward
    out_ref[...] = jnp.zeros_like(out_ref)
    out_ref[pl.ds(2 * CAP, orbits, stride=MSG), :] = jnp.broadcast_to(
        row_of_scalars([total(field * forward)]), (orbits, LANES)
    )
    spread(field, field_ref)
    transposed_products(footprint_ref, field_ref, out_ref, meta_ref, 0, footprint_ref.shape[0])


def call(kernel, out_shape, kinds, out_kinds=None, scratch=()):
    spaces = {"v": pltpu.VMEM, "s": pltpu.SMEM, "h": pl.ANY}
    single = not isinstance(out_shape, (list, tuple))
    out_kinds = out_kinds or "v" * (1 if single else len(out_shape))
    out_specs = [pl.BlockSpec(memory_space=spaces[kind]) for kind in out_kinds]
    return pl.pallas_call(
        kernel,
        out_shape=out_shape,
        in_specs=[pl.BlockSpec(memory_space=spaces[kind]) for kind in kinds],
        out_specs=out_specs[0] if single else out_specs,
        scratch_shapes=list(scratch),
        compiler_params=pltpu.CompilerParams(vmem_limit_bytes=32 * 1024 * 1024),
    )


def per_device(observed, weights, precision_prior, footprint, block_rows, block_cells):
    rows, soundings = observed.shape
    cells, width = precision_prior.shape
    blocks = footprint.shape[0]
    orbits = lax.axis_size("orb")
    reps = lax.axis_size("rep")
    shape = jax.ShapeDtypeStruct
    messages = shape((orbits * MSG, LANES), F32)
    packed_shape = shape((8, soundings * rows // 8), F32)
    scalar_shape = shape((8, LANES), F32)
    region = shape((cells, width), F32)
    field = pltpu.VMEM((rows, soundings, LANES), F32)

    def exchange(array):
        array = array.reshape(orbits, 1, MSG * LANES)
        array = lax.all_to_all(array, "orb", split_axis=0, concat_axis=0, tiled=True)
        return array.reshape(messages.shape)

    in_hbm = [
        pltpu.with_memory_space_constraint(array, pltpu.HBM)
        for array in (block_rows, block_cells, observed, weights, footprint)
    ]
    outgoing, meta, packed_weights, footprint = call(
        functools.partial(start_kernel, cells),
        [
            messages,
            pltpu.SMEM((2 * blocks,), jnp.int32),
            packed_shape,
            pltpu.VMEM(footprint.shape, footprint.dtype),
        ],
        "hhhhh",
        "vsvv",
        [
            field,
            pltpu.SMEM((orbits,), jnp.int32),
            pltpu.SMEM((blocks,), jnp.int32),
            pltpu.SMEM((blocks,), jnp.int32),
            pltpu.VMEM(observed.shape, F32),
            pltpu.VMEM(weights.shape, F32),
            pltpu.SemaphoreType.DMA((4,)),
            pltpu.SemaphoreType.DMA((6,)),
        ],
    )(*in_hbm)
    incoming = exchange(outgoing)
    residual, outgoing, collect, pick = call(
        first_owner_kernel,
        [
            region,
            messages,
            shape((cells, 3 * CAP * orbits), BF16),
            shape((CAP * orbits, LANES), BF16),
        ],
        "vv",
    )(incoming, precision_prior)
    direction = solution = residual
    image = jnp.zeros(packed_shape.shape, F32)
    scalars = jnp.zeros(scalar_shape.shape, F32)
    for iteration in range(ITERS):
        first, last = iteration == 0, iteration == ITERS - 1
        partial = call(
            forward_kernel,
            shape((reps, 24, LANES), F32),
            "svv",
            scratch=[field],
        )(meta, exchange(outgoing), footprint)
        partial = lax.all_to_all(partial, "rep", split_axis=0, concat_axis=0, tiled=True)
        outgoing, image, scalars = call(
            functools.partial(adjoint_kernel, first),
            [messages, packed_shape, scalar_shape],
            "svvvvv",
            scratch=[field],
        )(meta, partial, packed_weights, footprint, image, scalars)
        incoming = exchange(outgoing)
        results = call(
            functools.partial(owner_kernel, last, first),
            [region, region] if last else [region, region, region, messages],
            "vvvvvvvv",
        )(incoming, scalars, precision_prior, collect, pick, residual, direction, solution)
        residual, solution = results[:2]
        if not last:
            direction, outgoing = results[2:]
    return (solution, residual)


def solution(mesh):
    in_specs = (
        P("orb", None),
        P("orb", None),
        P("orb", "rep"),
        P("orb", None, "rep"),
        P("orb"),
        P("orb"),
    )
    out_specs = (P("orb", "rep"), P("orb", "rep"))
    return jax.shard_map(
        per_device, mesh=mesh, in_specs=in_specs, out_specs=out_specs, check_vma=False
    )
```

```python
import functools

import jax
import jax.numpy as jnp
from jax import lax
from jax.experimental import pallas as pl
from jax.experimental.pallas import tpu as pltpu
from jax.sharding import PartitionSpec as P

ITERS = 4
CORES = 2
CAP = 2 * CORES
FETCH = 2 * CAP
DELIVER = FETCH + 1
LANES = 128
SUB = 16
F32 = jnp.float32
BF16 = jnp.bfloat16


def lane_ids(shape):
    return lax.broadcasted_iota(jnp.int32, shape, len(shape) - 1)


def three_parts(values):
    high = values.astype(BF16)
    rest = values - high.astype(F32)
    middle = rest.astype(BF16)
    low = (rest - middle.astype(F32)).astype(BF16)
    return high, middle, low


def spread(packed, field_ref):
    rows, soundings, _ = field_ref.shape
    for group in range(soundings // 8):
        for row in range(rows):
            lane = rows * group + row
            field_ref[row, 8 * group : 8 * group + 8, :] = jnp.broadcast_to(
                packed[:, lane : lane + 1], (8, LANES)
            )


def transposed_product(footprint_ref, field_ref, out_ref, block, row, place):
    soundings = footprint_ref.shape[1]
    left = jnp.zeros((SUB, LANES), F32)
    right = jnp.zeros((SUB, LANES), F32)
    for start in range(0, soundings, SUB):
        part = footprint_ref[block, start : start + SUB, :].astype(F32)
        z = field_ref[row, start : start + SUB, :]
        left = left + part[:, :LANES] * z
        right = right + part[:, LANES:] * z
    out_ref[pl.ds(place, 1), :] = jnp.sum(left, axis=0, keepdims=True)
    out_ref[pl.ds(place + 1, 1), :] = jnp.sum(right, axis=0, keepdims=True)


def each(first, last, together, do):
    def body(step, carry):
        for at in range(together):
            do(first + step * together + at)
        return carry

    lax.fori_loop(0, (last - first) // together, body, 0)


def in_columns(values):
    rows, soundings = values.shape
    parts = []
    for start in range(0, soundings, LANES):
        part = values[:, start : start + LANES]
        parts.append(jnp.concatenate([part] * (LANES // rows), axis=0).T)
    return jnp.concatenate(parts, axis=0)


def start_kernel(
    cells, rows_hbm, cells_hbm, observed_hbm, weights_hbm, footprint_hbm,
    out_ref, meta_ref, packed_ref, footprint_ref,
    field_ref, count_ref, rows_ref, cells_ref, observed_ref, weights_ref, sems, chunk_sems
):
    blocks = footprint_ref.shape[0]
    rows, soundings = weights_ref.shape
    peers = out_ref.shape[0] // DELIVER
    chunks = chunk_sems.shape[0]
    size = blocks // chunks
    small = [
        pltpu.make_async_copy(source, target, sems.at[at])
        for at, (source, target) in enumerate(
            [
                (rows_hbm, rows_ref),
                (cells_hbm, cells_ref),
                (observed_hbm, observed_ref),
                (weights_hbm, weights_ref),
            ]
        )
    ]
    for copy in small:
        copy.start()
    large = []
    for chunk in range(chunks):
        span = pl.ds(chunk * size, size)
        large.append(
            pltpu.make_async_copy(footprint_hbm.at[span], footprint_ref.at[span], chunk_sems.at[chunk])
        )
        large[-1].start()
    out_ref[...] = jnp.zeros_like(out_ref)
    for peer in range(peers):
        count_ref[peer] = 0
    for copy in small:
        copy.wait()
    weights = weights_ref[...]
    columns = in_columns(weights * observed_ref[...])
    for row in range(rows):
        field_ref[row] = jnp.broadcast_to(columns[:, row : row + 1], (soundings, LANES))
    columns = in_columns(weights)
    groups = LANES // rows
    lanes = lane_ids((8, LANES)) // rows
    for half in range(soundings // LANES):
        packed = jnp.zeros((8, LANES), F32)
        for at in range(groups):
            start = half * LANES + 8 * at
            packed = jnp.where(lanes == at, columns[start : start + 8, :], packed)
        packed_ref[:, half * LANES : (half + 1) * LANES] = packed

    def product(block):
        cell = cells_ref[block]
        peer = cell // cells
        slot = cell % cells
        rank = count_ref[peer]
        count_ref[peer] = rank + 1
        row = rows_ref[block] % rows
        place = peer * DELIVER + 2 * rank
        meta_ref[block] = place
        meta_ref[blocks + block] = row
        meta_ref[2 * blocks + block] = peer * FETCH + 2 * rank
        scalars = pl.ds(peer * DELIVER + FETCH, 1)
        out_ref[scalars, :] = jnp.where(
            lane_ids((1, LANES)) == rank, (slot + 1).astype(F32), out_ref[scalars, :]
        )
        transposed_product(footprint_ref, field_ref, out_ref, block, row, place)

    for chunk in range(chunks):
        large[chunk].wait()
        each(chunk * size, (chunk + 1) * size, 4, product)


def serve(residual, pick, out_ref):
    peers = out_ref.shape[0] // FETCH
    high, middle, low = three_parts(residual)
    stacked = jnp.concatenate([high, middle, low, jnp.zeros_like(high)], axis=0)
    pieces = jnp.dot(pick, stacked, preferred_element_type=F32)
    for slot in range(CAP):
        for half in range(2):
            out_ref[pl.ds(2 * slot + half, peers, stride=FETCH), :] = pieces[
                slot * peers : (slot + 1) * peers, half * LANES : (half + 1) * LANES
            ]


def gathered(in_ref, collect):
    peers = in_ref.shape[0] // DELIVER
    slots = [
        jnp.concatenate(
            [in_ref[pl.ds(2 * slot + half, peers, stride=DELIVER), :] for half in range(2)], axis=1
        )
        for slot in range(CAP)
    ]
    high, middle, low = three_parts(jnp.concatenate(slots, axis=0))
    return jnp.dot(collect, jnp.concatenate([high, middle, low], axis=0), preferred_element_type=F32)


def arrived_scalars(in_ref):
    peers = in_ref.shape[0] // DELIVER
    row = jnp.sum(in_ref[pl.ds(FETCH, peers, stride=DELIVER), :], axis=0, keepdims=True)
    return jnp.broadcast_to(row, (8, LANES))


def row_of_scalars(values):
    lanes = lane_ids((8, LANES))
    row = jnp.zeros((8, LANES), F32)
    for lane, value in enumerate(values):
        row = jnp.where(lanes == lane, value, row)
    return row


def total(values):
    return jnp.sum(jnp.sum(values, axis=0, keepdims=True), axis=1, keepdims=True)


def first_gather_kernel(in_ref, prior_ref, half_ref, collect_ref, pick_ref):
    peers = in_ref.shape[0] // DELIVER
    own, width = prior_ref.shape
    cells = CORES * own
    ids = in_ref[pl.ds(FETCH, peers, stride=DELIVER), :]
    lanes = lane_ids((peers, LANES)).astype(F32)
    pick = jnp.concatenate(
        [(ids[:, slot : slot + 1] == lanes + 1.0).astype(F32) for slot in range(CAP)], axis=0
    )
    pick = jnp.where(lane_ids(pick.shape) < cells, pick, 0.0)
    collect = jnp.concatenate([pick.T[:cells, :]] * 3, axis=1).astype(BF16)
    collect_ref[...] = collect
    folds = [pick[:, :cells]] * 3 + [jnp.zeros((pick.shape[0], cells), F32)]
    pick_ref[...] = jnp.concatenate(folds, axis=1).astype(BF16)
    half_ref[0:cells, :] = gathered(in_ref, collect)
    half_ref[cells : cells + own, :] = prior_ref[...]


def gather_kernel(in_ref, collect_ref, half_ref):
    cells = collect_ref.shape[0]
    half_ref[0:cells, :] = gathered(in_ref, collect_ref[...])
    scalars = arrived_scalars(in_ref)
    half_ref[cells : cells + 8, :] = jnp.concatenate([scalars, jnp.zeros_like(scalars)], axis=1)


def partial_sums(prior, residual, direction=None):
    values = [0.5 * residual * residual, 0.5 * prior * residual * residual]
    if direction is not None:
        values.append(0.5 * prior * residual * direction)
    return row_of_scalars([total(value) for value in values])


def first_update_kernel(mine_ref, other_ref, pick_ref, prior_ref, residual_ref, sums_ref, out_ref):
    cells = residual_ref.shape[0]
    own = cells // CORES
    first = lax.axis_index("orb") % CORES == 0
    mine = mine_ref[cells : cells + own, :]
    other = other_ref[cells : cells + own, :]
    prior = jnp.concatenate([jnp.where(first, mine, other), jnp.where(first, other, mine)], axis=0)
    prior_ref[...] = prior
    residual = mine_ref[0:cells, :] + other_ref[0:cells, :]
    residual_ref[...] = residual
    sums_ref[...] = partial_sums(prior, residual)
    serve(residual, pick_ref[...], out_ref)


def update_kernel(first, last, *refs):
    mine_ref, other_ref, pick_ref, prior_ref, residual_ref, *refs = refs
    if not first:
        state_ref, direction_ref, image_ref, solution_ref, *refs = refs
    cells = residual_ref.shape[0]
    sums = mine_ref[cells : cells + 1, :] + other_ref[cells : cells + 1, :]
    norm, prior_rr, prior_rd, forward_rr, forward_rd = [sums[:, at : at + 1] for at in range(5)]
    prior = prior_ref[...]
    residual = residual_ref[...]
    image = mine_ref[0:cells, :] + other_ref[0:cells, :] + prior * residual
    beta = jnp.zeros((1, 1), F32)
    direction, prior_dd, forward_dd = residual, prior_rr, forward_rr
    if not first:
        beta = norm / state_ref[0:1, 0:1]
        prior_dd = prior_rr + beta * (2.0 * prior_rd + beta * state_ref[0:1, 1:2])
        forward_dd = forward_rr + beta * (2.0 * forward_rd + beta * state_ref[0:1, 2:3])
        direction = residual + beta * direction_ref[...]
        image = image + beta * image_ref[...]
    alpha = norm / (prior_dd + forward_dd)
    solution = alpha * direction if first else solution_ref[...] + alpha * direction
    residual = residual - alpha * image
    if last:
        new_solution_ref, new_residual_ref = refs
        own = cells // CORES
        core_first = lax.axis_index("orb") % CORES == 0
        new_solution_ref[...] = jnp.where(core_first, solution[:own], solution[own:])
        new_residual_ref[...] = jnp.where(core_first, residual[:own], residual[own:])
        return
    new_residual_ref, sums_ref, out_ref, new_state_ref, new_direction_ref, new_image_ref, new_solution_ref = refs
    serve(residual, pick_ref[...], out_ref)
    sums_ref[...] = partial_sums(prior, residual, direction)
    new_residual_ref[...] = residual
    new_state_ref[...] = row_of_scalars([norm, prior_dd, forward_dd, beta])
    new_direction_ref[...] = direction
    new_image_ref[...] = image
    new_solution_ref[...] = solution


def forward_kernel(meta_ref, in_ref, scalars_ref, footprint_ref, out_ref, sums_ref):
    blocks = footprint_ref.shape[0]
    rows, soundings, _ = sums_ref.shape
    sums_ref[...] = jnp.zeros_like(sums_ref)

    def product(block):
        row = meta_ref[blocks + block]
        place = meta_ref[2 * blocks + block]
        left = jnp.broadcast_to(in_ref[pl.ds(place, 1), :], (SUB, LANES))
        right = jnp.broadcast_to(in_ref[pl.ds(place + 1, 1), :], (SUB, LANES))
        for start in range(0, soundings, SUB):
            part = footprint_ref[block, start : start + SUB, :].astype(F32)
            sums_ref[row, start : start + SUB, :] += part[:, :LANES] * left + part[:, LANES:] * right

    each(0, blocks, 4, product)
    lanes = lane_ids((8, LANES))
    per_half = LANES // rows
    halves = []
    for half in range(soundings // 8 // per_half):
        packed = [jnp.zeros((8, LANES), F32) for _ in range(4)]
        for at in range(per_half):
            group = half * per_half + at
            for row in range(rows):
                summed = jnp.sum(sums_ref[row, 8 * group : 8 * group + 8, :], axis=1, keepdims=True)
                packed[row % 4] = jnp.where(lanes == rows * at + row, summed, packed[row % 4])
        halves.append((packed[0] + packed[1]) + (packed[2] + packed[3]))
    halves.append(scalars_ref[...])
    message = jnp.concatenate(halves, axis=0)
    for peer in range(out_ref.shape[0]):
        out_ref[peer] = message


def adjoint_kernel(iteration, last, *refs):
    meta_ref, in_ref, weights_ref, footprint_ref, *refs = refs
    if iteration > 0:
        state_ref, old_ref, *refs = refs
    if iteration > 1:
        older_ref, *refs = refs
    out_ref, *refs = refs
    blocks = footprint_ref.shape[0]
    peers = out_ref.shape[0] // DELIVER
    summed = in_ref[0]
    for peer in range(1, in_ref.shape[0]):
        summed = summed + in_ref[peer]
    forward = jnp.concatenate([summed[0:8], summed[8:16]], axis=1)
    field = weights_ref[...] * forward
    *refs, field_ref = refs
    out_ref[...] = jnp.zeros_like(out_ref)
    spread(field, field_ref)
    lanes = lane_ids((8, LANES))
    scalars = jnp.where(lanes == 3, total(field * forward), summed[16:24])
    if iteration > 0:
        direction = old_ref[...]
        if iteration > 1:
            direction = direction + state_ref[0:1, 3:4] * older_ref[...]
        scalars = jnp.where(lanes == 4, total(field * direction), scalars)
    if not last:
        refs[0][...] = forward
        if iteration > 0:
            refs[1][...] = direction
    out_ref[pl.ds(FETCH, peers, stride=DELIVER), :] = jnp.broadcast_to(scalars[0:1], (peers, LANES))

    def product(block):
        transposed_product(
            footprint_ref, field_ref, out_ref, block, meta_ref[blocks + block], meta_ref[block]
        )

    each(0, blocks, 4, product)


def call(kernel, out_shape, kinds, out_kinds=None, scratch=()):
    spaces = {"v": pltpu.VMEM, "s": pltpu.SMEM, "h": pl.ANY}
    out_kinds = out_kinds or "v" * len(out_shape)
    return pl.pallas_call(
        kernel,
        out_shape=out_shape,
        in_specs=[pl.BlockSpec(memory_space=spaces[kind]) for kind in kinds],
        out_specs=[pl.BlockSpec(memory_space=spaces[kind]) for kind in out_kinds],
        scratch_shapes=list(scratch),
        compiler_params=pltpu.CompilerParams(vmem_limit_bytes=32 * 1024 * 1024),
    )


def per_device(observed, weights, precision_prior, footprint, block_rows, block_cells):
    rows, soundings = observed.shape
    own, width = precision_prior.shape
    cells = CORES * own
    blocks = footprint.shape[0]
    orbits = lax.axis_size("orb")
    reps = lax.axis_size("rep")
    peers = orbits // CORES
    shape = jax.ShapeDtypeStruct
    fetched = shape((peers * FETCH, LANES), F32)
    delivered = shape((peers * DELIVER, LANES), F32)
    packed_shape = shape((8, soundings * rows // 8), F32)
    scalar_shape = shape((8, LANES), F32)
    region = shape((cells, width), F32)
    field = pltpu.VMEM((rows, soundings, LANES), F32)
    same_core = [[CORES * peer + core for peer in range(peers)] for core in range(CORES)]
    swapped = [(device, device ^ 1) for device in range(orbits)]

    def exchange(array):
        flat = array.reshape(peers, 1, array.shape[0] // peers * LANES)
        flat = lax.all_to_all(
            flat, "orb", split_axis=0, concat_axis=0, axis_index_groups=same_core, tiled=True
        )
        return flat.reshape(array.shape)

    def swap(array):
        return lax.ppermute(array, "orb", swapped)

    in_hbm = [
        pltpu.with_memory_space_constraint(array, pltpu.HBM)
        for array in (block_rows, block_cells, observed, weights, footprint)
    ]
    outgoing, meta, packed_weights, footprint = call(
        functools.partial(start_kernel, cells),
        [
            delivered,
            pltpu.SMEM((3 * blocks,), jnp.int32),
            packed_shape,
            pltpu.VMEM(footprint.shape, footprint.dtype),
        ],
        "hhhhh",
        "vsvv",
        [
            field,
            pltpu.SMEM((peers,), jnp.int32),
            pltpu.SMEM((blocks,), jnp.int32),
            pltpu.SMEM((blocks,), jnp.int32),
            pltpu.VMEM(observed.shape, F32),
            pltpu.VMEM(weights.shape, F32),
            pltpu.SemaphoreType.DMA((4,)),
            pltpu.SemaphoreType.DMA((6,)),
        ],
    )(*in_hbm)
    half, collect, pick = call(
        first_gather_kernel,
        [
            shape((cells + own, width), F32),
            shape((cells, 3 * CAP * peers), BF16),
            shape((CAP * peers, 4 * cells), BF16),
        ],
        "vv",
    )(exchange(outgoing), precision_prior)
    prior, residual, sums, outgoing = call(
        first_update_kernel, [region, region, scalar_shape, fetched], "vvv"
    )(half, swap(half), pick)
    state, history, images = None, (), ()
    for iteration in range(ITERS):
        first, last = iteration == 0, iteration == ITERS - 1
        (partial,) = call(
            forward_kernel, [shape((reps, 24, LANES), F32)], "svvv", scratch=[field]
        )(meta, exchange(outgoing), sums, footprint)
        partial = lax.all_to_all(partial, "rep", split_axis=0, concat_axis=0, tiled=True)
        operands = [meta, partial, packed_weights, footprint]
        operands += [] if first else [state, *images]
        outgoing, *images = call(
            functools.partial(adjoint_kernel, iteration, last),
            [delivered] + ([] if last else [packed_shape] * (1 if first else 2)),
            "s" + "v" * (len(operands) - 1),
            scratch=[field],
        )(*operands)
        (half,) = call(gather_kernel, [shape((cells + 8, width), F32)], "vv")(
            exchange(outgoing), collect
        )
        operands = [half, swap(half), pick, prior, residual]
        operands += [] if first else [state, *history]
        results = call(
            functools.partial(update_kernel, first, last),
            [shape((own, width), F32)] * 2
            if last
            else [region, scalar_shape, fetched, scalar_shape, region, region, region],
            "v" * len(operands),
        )(*operands)
        if not last:
            residual, sums, outgoing, state, *history = results
    return tuple(results)


def solution(mesh):
    in_specs = (
        P("orb", None),
        P("orb", None),
        P("orb", "rep"),
        P("orb", None, "rep"),
        P("orb"),
        P("orb"),
    )
    out_specs = (P("orb", "rep"), P("orb", "rep"))
    return jax.shard_map(
        per_device, mesh=mesh, in_specs=in_specs, out_specs=out_specs, check_vma=False
    )
```

```python
import functools

import jax
import jax.numpy as jnp
from jax import lax
from jax.experimental import pallas as pl
from jax.experimental.pallas import tpu as pltpu
from jax.sharding import PartitionSpec as P

ITERS = 4
CORES = 2
CAP = 2 * CORES
FETCH = 2 * CAP
DELIVER = FETCH + 1
LANES = 128
SUB = 16
IN_FLIGHT = 6
F32 = jnp.float32
BF16 = jnp.bfloat16


def lane_ids(shape):
    return lax.broadcasted_iota(jnp.int32, shape, len(shape) - 1)


def three_parts(values):
    high = values.astype(BF16)
    rest = values - high.astype(F32)
    middle = rest.astype(BF16)
    low = (rest - middle.astype(F32)).astype(BF16)
    return high, middle, low


def spread(packed, field_ref):
    rows, soundings, _ = field_ref.shape
    for group in range(soundings // 8):
        for row in range(rows):
            lane = rows * group + row
            field_ref[row, 8 * group : 8 * group + 8, :] = jnp.broadcast_to(
                packed[:, lane : lane + 1], (8, LANES)
            )


def transposed_product(footprint_ref, field_ref, out_ref, block, row, place, keep_ref=None):
    soundings = footprint_ref.shape[1]
    left = jnp.zeros((SUB, LANES), F32)
    right = jnp.zeros((SUB, LANES), F32)
    for start in range(0, soundings, SUB):
        part = footprint_ref[block, start : start + SUB, :].astype(F32)
        if keep_ref is not None:
            keep_ref[block, start : start + SUB, :] = part
        z = field_ref[row, start : start + SUB, :]
        left = left + part[:, :LANES] * z
        right = right + part[:, LANES:] * z
    out_ref[pl.ds(place, 1), :] = jnp.sum(left, axis=0, keepdims=True)
    out_ref[pl.ds(place + 1, 1), :] = jnp.sum(right, axis=0, keepdims=True)


def each(first, last, together, do):
    def body(step, carry):
        for at in range(together):
            do(first + step * together + at)
        return carry

    lax.fori_loop(0, (last - first) // together, body, 0)


def in_columns(values):
    rows, soundings = values.shape
    parts = []
    for start in range(0, soundings, LANES):
        part = values[:, start : start + LANES]
        parts.append(jnp.concatenate([part] * (LANES // rows), axis=0).T)
    return jnp.concatenate(parts, axis=0)


def start_kernel(
    cells, rows_hbm, cells_hbm, observed_hbm, weights_hbm, footprint_hbm,
    out_ref, meta_ref, packed_ref, footprint_ref,
    arrived_ref, field_ref, count_ref, rows_ref, cells_ref, observed_ref, weights_ref, sems, chunk_sems
):
    blocks = footprint_ref.shape[0]
    rows, soundings = weights_ref.shape
    peers = out_ref.shape[0] // DELIVER
    chunks = chunk_sems.shape[0]
    size = blocks // chunks
    small = [
        pltpu.make_async_copy(source, target, sems.at[at])
        for at, (source, target) in enumerate(
            [
                (rows_hbm, rows_ref),
                (cells_hbm, cells_ref),
                (observed_hbm, observed_ref),
                (weights_hbm, weights_ref),
            ]
        )
    ]
    for copy in small:
        copy.start()
    large = []
    for chunk in range(chunks):
        span = pl.ds(chunk * size, size)
        large.append(
            pltpu.make_async_copy(footprint_hbm.at[span], arrived_ref.at[span], chunk_sems.at[chunk])
        )
    for copy in large[:IN_FLIGHT]:
        copy.start()
    out_ref[...] = jnp.zeros_like(out_ref)
    for peer in range(peers):
        count_ref[peer] = 0
    for copy in small:
        copy.wait()
    weights = weights_ref[...]
    columns = in_columns(weights * observed_ref[...])
    for row in range(rows):
        field_ref[row] = jnp.broadcast_to(columns[:, row : row + 1], (soundings, LANES))
    columns = in_columns(weights)
    groups = LANES // rows
    lanes = lane_ids((8, LANES)) // rows
    for half in range(soundings // LANES):
        packed = jnp.zeros((8, LANES), F32)
        for at in range(groups):
            start = half * LANES + 8 * at
            packed = jnp.where(lanes == at, columns[start : start + 8, :], packed)
        packed_ref[:, half * LANES : (half + 1) * LANES] = packed

    def product(block):
        cell = cells_ref[block]
        peer = cell // cells
        slot = cell % cells
        rank = count_ref[peer]
        count_ref[peer] = rank + 1
        row = rows_ref[block] % rows
        place = peer * DELIVER + 2 * rank
        meta_ref[block] = place
        meta_ref[blocks + block] = row
        meta_ref[2 * blocks + block] = peer * FETCH + 2 * rank
        scalars = pl.ds(peer * DELIVER + FETCH, 1)
        out_ref[scalars, :] = jnp.where(
            lane_ids((1, LANES)) == rank, (slot + 1).astype(F32), out_ref[scalars, :]
        )
        transposed_product(arrived_ref, field_ref, out_ref, block, row, place, footprint_ref)

    for chunk in range(chunks):
        large[chunk].wait()
        if chunk + IN_FLIGHT < chunks:
            large[chunk + IN_FLIGHT].start()
        each(chunk * size, (chunk + 1) * size, 4, product)


def serve(residual, pick, out_ref):
    peers = out_ref.shape[0] // FETCH
    high, middle, low = three_parts(residual)
    stacked = jnp.concatenate([high, middle, low, jnp.zeros_like(high)], axis=0)
    pieces = jnp.dot(pick, stacked, preferred_element_type=F32)
    for slot in range(CAP):
        for half in range(2):
            out_ref[pl.ds(2 * slot + half, peers, stride=FETCH), :] = pieces[
                slot * peers : (slot + 1) * peers, half * LANES : (half + 1) * LANES
            ]


def gathered(in_ref, collect):
    peers = in_ref.shape[0] // DELIVER
    slots = [
        jnp.concatenate(
            [in_ref[pl.ds(2 * slot + half, peers, stride=DELIVER), :] for half in range(2)], axis=1
        )
        for slot in range(CAP)
    ]
    high, middle, low = three_parts(jnp.concatenate(slots, axis=0))
    return jnp.dot(collect, jnp.concatenate([high, middle, low], axis=0), preferred_element_type=F32)


def arrived_scalars(in_ref):
    peers = in_ref.shape[0] // DELIVER
    row = jnp.sum(in_ref[pl.ds(FETCH, peers, stride=DELIVER), :], axis=0, keepdims=True)
    return jnp.broadcast_to(row, (8, LANES))


def row_of_scalars(values):
    lanes = lane_ids((8, LANES))
    row = jnp.zeros((8, LANES), F32)
    for lane, value in enumerate(values):
        row = jnp.where(lanes == lane, value, row)
    return row


def total(values):
    return jnp.sum(jnp.sum(values, axis=0, keepdims=True), axis=1, keepdims=True)


def first_gather_kernel(in_ref, prior_ref, half_ref, collect_ref, pick_ref):
    peers = in_ref.shape[0] // DELIVER
    own, width = prior_ref.shape
    cells = CORES * own
    ids = in_ref[pl.ds(FETCH, peers, stride=DELIVER), :]
    lanes = lane_ids((peers, LANES)).astype(F32)
    pick = jnp.concatenate(
        [(ids[:, slot : slot + 1] == lanes + 1.0).astype(F32) for slot in range(CAP)], axis=0
    )
    pick = jnp.where(lane_ids(pick.shape) < cells, pick, 0.0)
    collect = jnp.concatenate([pick.T[:cells, :]] * 3, axis=1).astype(BF16)
    collect_ref[...] = collect
    folds = [pick[:, :cells]] * 3 + [jnp.zeros((pick.shape[0], cells), F32)]
    pick_ref[...] = jnp.concatenate(folds, axis=1).astype(BF16)
    half_ref[0:cells, :] = gathered(in_ref, collect)
    half_ref[cells : cells + own, :] = prior_ref[...]


def gather_kernel(in_ref, collect_ref, half_ref):
    cells = collect_ref.shape[0]
    half_ref[0:cells, :] = gathered(in_ref, collect_ref[...])
    scalars = arrived_scalars(in_ref)
    half_ref[cells : cells + 8, :] = jnp.concatenate([scalars, jnp.zeros_like(scalars)], axis=1)


def partial_sums(prior, residual, direction=None):
    values = [0.5 * residual * residual, 0.5 * prior * residual * residual]
    if direction is not None:
        values.append(0.5 * prior * residual * direction)
    return row_of_scalars([total(value) for value in values])


def first_update_kernel(mine_ref, other_ref, pick_ref, prior_ref, residual_ref, out_ref):
    cells = residual_ref.shape[0]
    own = cells // CORES
    first = lax.axis_index("orb") % CORES == 0
    mine = mine_ref[cells : cells + own, :]
    other = other_ref[cells : cells + own, :]
    prior = jnp.concatenate([jnp.where(first, mine, other), jnp.where(first, other, mine)], axis=0)
    prior_ref[...] = prior
    residual = mine_ref[0:cells, :] + other_ref[0:cells, :]
    residual_ref[...] = residual
    serve(residual, pick_ref[...], out_ref)


def update_kernel(first, last, *refs):
    mine_ref, other_ref, pick_ref, prior_ref, residual_ref, *refs = refs
    if not first:
        state_ref, image_ref, *refs = refs
    if last:
        direction_ref, solution_ref, *refs = refs
    cells = residual_ref.shape[0]
    sums = mine_ref[cells : cells + 1, :] + other_ref[cells : cells + 1, :]
    norm, prior_rr, prior_rd, forward_rr, forward_rd = [sums[:, at : at + 1] for at in range(5)]
    residual = residual_ref[...]
    image = mine_ref[0:cells, :] + other_ref[0:cells, :] + prior_ref[...] * residual
    beta = jnp.zeros((1, 1), F32)
    prior_dd, forward_dd = prior_rr, forward_rr
    if not first:
        beta = norm / state_ref[0:1, 0:1]
        prior_dd = prior_rr + beta * (2.0 * prior_rd + beta * state_ref[0:1, 1:2])
        forward_dd = forward_rr + beta * (2.0 * forward_rd + beta * state_ref[0:1, 2:3])
        image = image + beta * image_ref[...]
    alpha = norm / (prior_dd + forward_dd)
    new_residual = residual - alpha * image
    if last:
        new_solution_ref, new_residual_ref = refs
        direction = residual + beta * direction_ref[...]
        solution = solution_ref[...] + alpha * direction
        own = cells // CORES
        core_first = lax.axis_index("orb") % CORES == 0
        new_solution_ref[...] = jnp.where(core_first, solution[:own], solution[own:])
        new_residual_ref[...] = jnp.where(core_first, new_residual[:own], new_residual[own:])
        return
    new_residual_ref, out_ref, new_state_ref, new_image_ref = refs
    serve(new_residual, pick_ref[...], out_ref)
    new_residual_ref[...] = new_residual
    new_state_ref[...] = row_of_scalars([norm, prior_dd, forward_dd, beta, alpha])
    new_image_ref[...] = image


def beside_kernel(first, state_ref, prior_ref, residual_ref, new_residual_ref, *refs):
    if not first:
        direction_ref, solution_ref, *refs = refs
    sums_ref, new_direction_ref, new_solution_ref = refs
    beta = state_ref[0:1, 3:4]
    alpha = state_ref[0:1, 4:5]
    direction = residual_ref[...]
    if not first:
        direction = direction + beta * direction_ref[...]
    solution = alpha * direction
    if not first:
        solution = solution + solution_ref[...]
    sums_ref[...] = partial_sums(prior_ref[...], new_residual_ref[...], direction)
    new_direction_ref[...] = direction
    new_solution_ref[...] = solution


def first_sums_kernel(prior_ref, residual_ref, sums_ref):
    sums_ref[...] = partial_sums(prior_ref[...], residual_ref[...])


def forward_kernel(meta_ref, in_ref, scalars_ref, footprint_ref, out_ref, sums_ref):
    blocks = footprint_ref.shape[0]
    rows, soundings, _ = sums_ref.shape
    sums_ref[...] = jnp.zeros_like(sums_ref)

    def product(block):
        row = meta_ref[blocks + block]
        place = meta_ref[2 * blocks + block]
        left = jnp.broadcast_to(in_ref[pl.ds(place, 1), :], (2 * SUB, LANES))
        right = jnp.broadcast_to(in_ref[pl.ds(place + 1, 1), :], (2 * SUB, LANES))
        for start in range(0, soundings, 2 * SUB):
            part = footprint_ref[block, start : start + 2 * SUB, :]
            sums_ref[row, start : start + 2 * SUB, :] += part[:, :LANES] * left + part[:, LANES:] * right

    each(0, blocks, 4, product)
    lanes = lane_ids((8, LANES))
    per_half = LANES // rows
    halves = []
    for half in range(soundings // 8 // per_half):
        packed = [jnp.zeros((8, LANES), F32) for _ in range(4)]
        for at in range(per_half):
            group = half * per_half + at
            for row in range(rows):
                summed = jnp.sum(sums_ref[row, 8 * group : 8 * group + 8, :], axis=1, keepdims=True)
                packed[row % 4] = jnp.where(lanes == rows * at + row, summed, packed[row % 4])
        halves.append((packed[0] + packed[1]) + (packed[2] + packed[3]))
    halves.append(scalars_ref[...])
    message = jnp.concatenate(halves, axis=0)
    for peer in range(out_ref.shape[0]):
        out_ref[peer] = message


def adjoint_kernel(iteration, last, *refs):
    meta_ref, in_ref, weights_ref, footprint_ref, *refs = refs
    if iteration > 0:
        state_ref, old_ref, *refs = refs
    if iteration > 1:
        older_ref, *refs = refs
    out_ref, *refs = refs
    blocks = footprint_ref.shape[0]
    peers = out_ref.shape[0] // DELIVER
    summed = in_ref[0]
    for peer in range(1, in_ref.shape[0]):
        summed = summed + in_ref[peer]
    forward = jnp.concatenate([summed[0:8], summed[8:16]], axis=1)
    field = weights_ref[...] * forward
    *refs, field_ref = refs
    out_ref[...] = jnp.zeros_like(out_ref)
    spread(field, field_ref)
    lanes = lane_ids((8, LANES))
    scalars = jnp.where(lanes == 3, total(field * forward), summed[16:24])
    if iteration > 0:
        direction = old_ref[...]
        if iteration > 1:
            direction = direction + state_ref[0:1, 3:4] * older_ref[...]
        scalars = jnp.where(lanes == 4, total(field * direction), scalars)
    if not last:
        refs[0][...] = forward
        if iteration > 0:
            refs[1][...] = direction
    out_ref[pl.ds(FETCH, peers, stride=DELIVER), :] = jnp.broadcast_to(scalars[0:1], (peers, LANES))

    def product(block):
        transposed_product(
            footprint_ref, field_ref, out_ref, block, meta_ref[blocks + block], meta_ref[block]
        )

    each(0, blocks, 8, product)


def call(kernel, out_shape, kinds, out_kinds=None, scratch=()):
    spaces = {"v": pltpu.VMEM, "s": pltpu.SMEM, "h": pl.ANY}
    out_kinds = out_kinds or "v" * len(out_shape)
    return pl.pallas_call(
        kernel,
        out_shape=out_shape,
        in_specs=[pl.BlockSpec(memory_space=spaces[kind]) for kind in kinds],
        out_specs=[pl.BlockSpec(memory_space=spaces[kind]) for kind in out_kinds],
        scratch_shapes=list(scratch),
        compiler_params=pltpu.CompilerParams(vmem_limit_bytes=16 * 1024 * 1024),
    )


def per_device(observed, weights, precision_prior, footprint, block_rows, block_cells):
    rows, soundings = observed.shape
    own, width = precision_prior.shape
    cells = CORES * own
    blocks = footprint.shape[0]
    orbits = lax.axis_size("orb")
    reps = lax.axis_size("rep")
    peers = orbits // CORES
    shape = jax.ShapeDtypeStruct
    fetched = shape((peers * FETCH, LANES), F32)
    delivered = shape((peers * DELIVER, LANES), F32)
    packed_shape = shape((8, soundings * rows // 8), F32)
    scalar_shape = shape((8, LANES), F32)
    region = shape((cells, width), F32)
    field = pltpu.VMEM((rows, soundings, LANES), F32)
    same_core = [[CORES * peer + core for peer in range(peers)] for core in range(CORES)]
    swapped = [(device, device ^ 1) for device in range(orbits)]

    def exchange(array):
        flat = array.reshape(peers, 1, array.shape[0] // peers * LANES)
        flat = lax.all_to_all(
            flat, "orb", split_axis=0, concat_axis=0, axis_index_groups=same_core, tiled=True
        )
        return flat.reshape(array.shape)

    def swap(array):
        return lax.ppermute(array, "orb", swapped)

    in_hbm = [
        pltpu.with_memory_space_constraint(array, pltpu.HBM)
        for array in (block_rows, block_cells, observed, weights, footprint)
    ]
    outgoing, meta, packed_weights, footprint = call(
        functools.partial(start_kernel, cells),
        [
            delivered,
            pltpu.SMEM((3 * blocks,), jnp.int32),
            packed_shape,
            pltpu.VMEM(footprint.shape, F32),
        ],
        "hhhhh",
        "vsvv",
        [
            pltpu.VMEM(footprint.shape, footprint.dtype),
            field,
            pltpu.SMEM((peers,), jnp.int32),
            pltpu.SMEM((blocks,), jnp.int32),
            pltpu.SMEM((blocks,), jnp.int32),
            pltpu.VMEM(observed.shape, F32),
            pltpu.VMEM(weights.shape, F32),
            pltpu.SemaphoreType.DMA((4,)),
            pltpu.SemaphoreType.DMA((12,)),
        ],
    )(*in_hbm)
    half, collect, pick = call(
        first_gather_kernel,
        [
            shape((cells + own, width), F32),
            shape((cells, 3 * CAP * peers), BF16),
            shape((CAP * peers, 4 * cells), BF16),
        ],
        "vv",
    )(exchange(outgoing), precision_prior)
    prior, residual, outgoing = call(first_update_kernel, [region, region, fetched], "vvv")(
        half, swap(half), pick
    )
    incoming = exchange(outgoing)
    (sums,) = call(first_sums_kernel, [scalar_shape], "vv")(prior, residual)
    state, history, images, moved = None, [], [], []
    for iteration in range(ITERS):
        first, last = iteration == 0, iteration == ITERS - 1
        (partial,) = call(
            forward_kernel, [shape((reps, 24, LANES), F32)], "svvv", scratch=[field]
        )(meta, incoming, sums, footprint)
        partial = lax.all_to_all(partial, "rep", split_axis=0, concat_axis=0, tiled=True)
        operands = [meta, partial, packed_weights, footprint]
        operands += [] if first else [state, *images]
        outgoing, *images = call(
            functools.partial(adjoint_kernel, iteration, last),
            [delivered] + ([] if last else [packed_shape] * (1 if first else 2)),
            "s" + "v" * (len(operands) - 1),
            scratch=[field],
        )(*operands)
        (half,) = call(gather_kernel, [shape((cells + 8, width), F32)], "vv")(
            exchange(outgoing), collect
        )
        operands = [half, swap(half), pick, prior, residual]
        operands += [] if first else [state, *moved]
        operands += history if last else []
        results = call(
            functools.partial(update_kernel, first, last),
            [shape((own, width), F32)] * 2 if last else [region, fetched, scalar_shape, region],
            "v" * len(operands),
        )(*operands)
        if not last:
            new_residual, outgoing, state, *moved = results
            incoming = exchange(outgoing)
            operands = [state, prior, residual, new_residual, *history]
            sums, *history = call(
                functools.partial(beside_kernel, first),
                [scalar_shape, region, region],
                "v" * len(operands),
            )(*operands)
            residual = new_residual
    return tuple(results)


def solution(mesh):
    in_specs = (
        P("orb", None),
        P("orb", None),
        P("orb", "rep"),
        P("orb", None, "rep"),
        P("orb"),
        P("orb"),
    )
    out_specs = (P("orb", "rep"), P("orb", "rep"))
    return jax.shard_map(
        per_device, mesh=mesh, in_specs=in_specs, out_specs=out_specs, check_vma=False
    )
```

```python
import functools

import jax
import jax.numpy as jnp
from jax import lax
from jax.experimental import pallas as pl
from jax.experimental.pallas import tpu as pltpu
from jax.sharding import PartitionSpec as P

ITERS = 4
CORES = 2
CAP = 2 * CORES
FETCH = 2 * CAP
DELIVER = FETCH + 1
LANES = 128
SUB = 16
IN_FLIGHT = 6
F32 = jnp.float32
BF16 = jnp.bfloat16


def lane_ids(shape):
    return lax.broadcasted_iota(jnp.int32, shape, len(shape) - 1)


def three_parts(values):
    high = values.astype(BF16)
    rest = values - high.astype(F32)
    middle = rest.astype(BF16)
    low = (rest - middle.astype(F32)).astype(BF16)
    return high, middle, low


def spread(packed, field_ref):
    rows, soundings, _ = field_ref.shape
    for group in range(soundings // 8):
        for row in range(rows):
            lane = rows * group + row
            field_ref[row, 8 * group : 8 * group + 8, :] = jnp.broadcast_to(
                packed[:, lane : lane + 1], (8, LANES)
            )


def transposed_product(footprint_ref, field_ref, out_ref, block, row, place, keep_ref=None):
    soundings = footprint_ref.shape[1]
    left = jnp.zeros((SUB, LANES), F32)
    right = jnp.zeros((SUB, LANES), F32)
    for start in range(0, soundings, SUB):
        part = footprint_ref[block, start : start + SUB, :].astype(F32)
        if keep_ref is not None:
            keep_ref[block, start : start + SUB, :] = part
        z = field_ref[row, start : start + SUB, :]
        left = left + part[:, :LANES] * z
        right = right + part[:, LANES:] * z
    out_ref[pl.ds(place, 1), :] = jnp.sum(left, axis=0, keepdims=True)
    out_ref[pl.ds(place + 1, 1), :] = jnp.sum(right, axis=0, keepdims=True)


def each(first, last, together, do):
    def body(step, carry):
        for at in range(together):
            do(first + step * together + at)
        return carry

    lax.fori_loop(0, (last - first) // together, body, 0)


def in_columns(values):
    rows, soundings = values.shape
    parts = []
    for start in range(0, soundings, LANES):
        part = values[:, start : start + LANES]
        parts.append(jnp.concatenate([part] * (LANES // rows), axis=0).T)
    return jnp.concatenate(parts, axis=0)


def start_kernel(
    cells, rows_hbm, cells_hbm, observed_hbm, weights_hbm, footprint_hbm,
    out_ref, meta_ref, packed_ref, footprint_ref,
    arrived_ref, field_ref, count_ref, rows_ref, cells_ref, observed_ref, weights_ref, sems, chunk_sems
):
    blocks = footprint_ref.shape[0]
    rows, soundings = weights_ref.shape
    peers = out_ref.shape[0] // DELIVER
    chunks = chunk_sems.shape[0]
    size = blocks // chunks
    small = [
        pltpu.make_async_copy(source, target, sems.at[at])
        for at, (source, target) in enumerate(
            [
                (rows_hbm, rows_ref),
                (cells_hbm, cells_ref),
                (observed_hbm, observed_ref),
                (weights_hbm, weights_ref),
            ]
        )
    ]
    for copy in small:
        copy.start()
    large = []
    for chunk in range(chunks):
        span = pl.ds(chunk * size, size)
        large.append(
            pltpu.make_async_copy(footprint_hbm.at[span], arrived_ref.at[span], chunk_sems.at[chunk])
        )
    for copy in large[:IN_FLIGHT]:
        copy.start()
    out_ref[...] = jnp.zeros_like(out_ref)
    for peer in range(peers):
        count_ref[peer] = 0
    for copy in small:
        copy.wait()
    weights = weights_ref[...]
    columns = in_columns(weights * observed_ref[...])
    for row in range(rows):
        field_ref[row] = jnp.broadcast_to(columns[:, row : row + 1], (soundings, LANES))
    columns = in_columns(weights)
    groups = LANES // rows
    lanes = lane_ids((8, LANES)) // rows
    for half in range(soundings // LANES):
        packed = jnp.zeros((8, LANES), F32)
        for at in range(groups):
            start = half * LANES + 8 * at
            packed = jnp.where(lanes == at, columns[start : start + 8, :], packed)
        packed_ref[:, half * LANES : (half + 1) * LANES] = packed

    def product(block):
        cell = cells_ref[block]
        peer = cell // cells
        slot = cell % cells
        rank = count_ref[peer]
        count_ref[peer] = rank + 1
        row = rows_ref[block] % rows
        place = peer * DELIVER + 2 * rank
        meta_ref[block] = place
        meta_ref[blocks + block] = row
        meta_ref[2 * blocks + block] = peer * FETCH + 2 * rank
        scalars = pl.ds(peer * DELIVER + FETCH, 1)
        out_ref[scalars, :] = jnp.where(
            lane_ids((1, LANES)) == rank, (slot + 1).astype(F32), out_ref[scalars, :]
        )
        transposed_product(arrived_ref, field_ref, out_ref, block, row, place, footprint_ref)

    for chunk in range(chunks):
        large[chunk].wait()
        if chunk + IN_FLIGHT < chunks:
            large[chunk + IN_FLIGHT].start()
        each(chunk * size, (chunk + 1) * size, 4, product)


def serve(residual, pick, out_ref):
    peers = out_ref.shape[0] // FETCH
    high, middle, low = three_parts(residual)
    stacked = jnp.concatenate([high, middle, low, jnp.zeros_like(high)], axis=0)
    pieces = jnp.dot(pick, stacked, preferred_element_type=F32)
    for slot in range(CAP):
        for half in range(2):
            out_ref[pl.ds(2 * slot + half, peers, stride=FETCH), :] = pieces[
                slot * peers : (slot + 1) * peers, half * LANES : (half + 1) * LANES
            ]


def gathered(in_ref, collect):
    peers = in_ref.shape[0] // DELIVER
    slots = [
        jnp.concatenate(
            [in_ref[pl.ds(2 * slot + half, peers, stride=DELIVER), :] for half in range(2)], axis=1
        )
        for slot in range(CAP)
    ]
    high, middle, low = three_parts(jnp.concatenate(slots, axis=0))
    return jnp.dot(collect, jnp.concatenate([high, middle, low], axis=0), preferred_element_type=F32)


def arrived_scalars(in_ref):
    peers = in_ref.shape[0] // DELIVER
    row = jnp.sum(in_ref[pl.ds(FETCH, peers, stride=DELIVER), :], axis=0, keepdims=True)
    return jnp.broadcast_to(row, (8, LANES))


def row_of_scalars(values):
    lanes = lane_ids((8, LANES))
    row = jnp.zeros((8, LANES), F32)
    for lane, value in enumerate(values):
        row = jnp.where(lanes == lane, value, row)
    return row


def total(values):
    return jnp.sum(jnp.sum(values, axis=0, keepdims=True), axis=1, keepdims=True)


def first_gather_kernel(in_ref, prior_ref, half_ref, collect_ref, pick_ref):
    peers = in_ref.shape[0] // DELIVER
    own, width = prior_ref.shape
    cells = CORES * own
    ids = in_ref[pl.ds(FETCH, peers, stride=DELIVER), :]
    lanes = lane_ids((peers, LANES)).astype(F32)
    pick = jnp.concatenate(
        [(ids[:, slot : slot + 1] == lanes + 1.0).astype(F32) for slot in range(CAP)], axis=0
    )
    pick = jnp.where(lane_ids(pick.shape) < cells, pick, 0.0)
    collect = jnp.concatenate([pick.T[:cells, :]] * 3, axis=1).astype(BF16)
    collect_ref[...] = collect
    folds = [pick[:, :cells]] * 3 + [jnp.zeros((pick.shape[0], cells), F32)]
    pick_ref[...] = jnp.concatenate(folds, axis=1).astype(BF16)
    half_ref[0:cells, :] = gathered(in_ref, collect)
    half_ref[cells : cells + own, :] = prior_ref[...]


def gather_kernel(in_ref, collect_ref, half_ref):
    cells = collect_ref.shape[0]
    half_ref[0:cells, :] = gathered(in_ref, collect_ref[...])
    scalars = arrived_scalars(in_ref)
    half_ref[cells : cells + 8, :] = jnp.concatenate([scalars, jnp.zeros_like(scalars)], axis=1)


def partial_sums(prior, residual, direction=None):
    values = [0.5 * residual * residual, 0.5 * prior * residual * residual]
    if direction is not None:
        values.append(0.5 * prior * residual * direction)
    return row_of_scalars([total(value) for value in values])


def first_update_kernel(mine_ref, other_ref, pick_ref, prior_ref, residual_ref, sums_ref, out_ref):
    cells = residual_ref.shape[0]
    own = cells // CORES
    first = lax.axis_index("orb") % CORES == 0
    mine = mine_ref[cells : cells + own, :]
    other = other_ref[cells : cells + own, :]
    prior = jnp.concatenate([jnp.where(first, mine, other), jnp.where(first, other, mine)], axis=0)
    prior_ref[...] = prior
    residual = mine_ref[0:cells, :] + other_ref[0:cells, :]
    residual_ref[...] = residual
    sums_ref[...] = partial_sums(prior, residual)
    serve(residual, pick_ref[...], out_ref)


def update_kernel(first, last, *refs):
    mine_ref, other_ref, pick_ref, prior_ref, residual_ref, *refs = refs
    if not first:
        state_ref, direction_ref, image_ref, solution_ref, *refs = refs
    cells = residual_ref.shape[0]
    sums = mine_ref[cells : cells + 1, :] + other_ref[cells : cells + 1, :]
    norm, prior_rr, prior_rd, forward_rr, forward_rd = [sums[:, at : at + 1] for at in range(5)]
    prior = prior_ref[...]
    residual = residual_ref[...]
    image = mine_ref[0:cells, :] + other_ref[0:cells, :] + prior * residual
    beta = jnp.zeros((1, 1), F32)
    direction, prior_dd, forward_dd = residual, prior_rr, forward_rr
    if not first:
        beta = norm / state_ref[0:1, 0:1]
        prior_dd = prior_rr + beta * (2.0 * prior_rd + beta * state_ref[0:1, 1:2])
        forward_dd = forward_rr + beta * (2.0 * forward_rd + beta * state_ref[0:1, 2:3])
        direction = residual + beta * direction_ref[...]
        image = image + beta * image_ref[...]
    alpha = norm / (prior_dd + forward_dd)
    solution = alpha * direction if first else solution_ref[...] + alpha * direction
    residual = residual - alpha * image
    if last:
        new_solution_ref, new_residual_ref = refs
        own = cells // CORES
        core_first = lax.axis_index("orb") % CORES == 0
        new_solution_ref[...] = jnp.where(core_first, solution[:own], solution[own:])
        new_residual_ref[...] = jnp.where(core_first, residual[:own], residual[own:])
        return
    new_residual_ref, sums_ref, out_ref, new_state_ref, new_direction_ref, new_image_ref, new_solution_ref = refs
    serve(residual, pick_ref[...], out_ref)
    sums_ref[...] = partial_sums(prior, residual, direction)
    new_residual_ref[...] = residual
    new_state_ref[...] = row_of_scalars([norm, prior_dd, forward_dd, beta])
    new_direction_ref[...] = direction
    new_image_ref[...] = image
    new_solution_ref[...] = solution


def forward_kernel(meta_ref, in_ref, scalars_ref, footprint_ref, out_ref, sums_ref):
    blocks = footprint_ref.shape[0]
    rows, soundings, _ = sums_ref.shape
    sums_ref[...] = jnp.zeros_like(sums_ref)

    def product(block):
        row = meta_ref[blocks + block]
        place = meta_ref[2 * blocks + block]
        left = jnp.broadcast_to(in_ref[pl.ds(place, 1), :], (2 * SUB, LANES))
        right = jnp.broadcast_to(in_ref[pl.ds(place + 1, 1), :], (2 * SUB, LANES))
        for start in range(0, soundings, 2 * SUB):
            part = footprint_ref[block, start : start + 2 * SUB, :]
            sums_ref[row, start : start + 2 * SUB, :] += part[:, :LANES] * left + part[:, LANES:] * right

    each(0, blocks, 4, product)
    lanes = lane_ids((8, LANES))
    per_half = LANES // rows
    halves = []
    for half in range(soundings // 8 // per_half):
        packed = [jnp.zeros((8, LANES), F32) for _ in range(4)]
        for at in range(per_half):
            group = half * per_half + at
            for row in range(rows):
                summed = jnp.sum(sums_ref[row, 8 * group : 8 * group + 8, :], axis=1, keepdims=True)
                packed[row % 4] = jnp.where(lanes == rows * at + row, summed, packed[row % 4])
        halves.append((packed[0] + packed[1]) + (packed[2] + packed[3]))
    halves.append(scalars_ref[...])
    message = jnp.concatenate(halves, axis=0)
    for peer in range(out_ref.shape[0]):
        out_ref[peer] = message


def adjoint_kernel(iteration, last, *refs):
    meta_ref, in_ref, weights_ref, footprint_ref, *refs = refs
    if iteration > 0:
        state_ref, old_ref, *refs = refs
    if iteration > 1:
        older_ref, *refs = refs
    out_ref, *refs = refs
    blocks = footprint_ref.shape[0]
    peers = out_ref.shape[0] // DELIVER
    summed = in_ref[0]
    for peer in range(1, in_ref.shape[0]):
        summed = summed + in_ref[peer]
    forward = jnp.concatenate([summed[0:8], summed[8:16]], axis=1)
    field = weights_ref[...] * forward
    *refs, field_ref = refs
    out_ref[...] = jnp.zeros_like(out_ref)
    spread(field, field_ref)
    lanes = lane_ids((8, LANES))
    scalars = jnp.where(lanes == 3, total(field * forward), summed[16:24])
    if iteration > 0:
        direction = old_ref[...]
        if iteration > 1:
            direction = direction + state_ref[0:1, 3:4] * older_ref[...]
        scalars = jnp.where(lanes == 4, total(field * direction), scalars)
    if not last:
        refs[0][...] = forward
        if iteration > 0:
            refs[1][...] = direction
    out_ref[pl.ds(FETCH, peers, stride=DELIVER), :] = jnp.broadcast_to(scalars[0:1], (peers, LANES))

    def product(block):
        transposed_product(
            footprint_ref, field_ref, out_ref, block, meta_ref[blocks + block], meta_ref[block]
        )

    each(0, blocks, 8, product)


def call(kernel, out_shape, kinds, out_kinds=None, scratch=()):
    spaces = {"v": pltpu.VMEM, "s": pltpu.SMEM, "h": pl.ANY}
    out_kinds = out_kinds or "v" * len(out_shape)
    return pl.pallas_call(
        kernel,
        out_shape=out_shape,
        in_specs=[pl.BlockSpec(memory_space=spaces[kind]) for kind in kinds],
        out_specs=[pl.BlockSpec(memory_space=spaces[kind]) for kind in out_kinds],
        scratch_shapes=list(scratch),
        compiler_params=pltpu.CompilerParams(vmem_limit_bytes=16 * 1024 * 1024),
    )


def per_device(observed, weights, precision_prior, footprint, block_rows, block_cells):
    rows, soundings = observed.shape
    own, width = precision_prior.shape
    cells = CORES * own
    blocks = footprint.shape[0]
    orbits = lax.axis_size("orb")
    reps = lax.axis_size("rep")
    peers = orbits // CORES
    shape = jax.ShapeDtypeStruct
    fetched = shape((peers * FETCH, LANES), F32)
    delivered = shape((peers * DELIVER, LANES), F32)
    packed_shape = shape((8, soundings * rows // 8), F32)
    scalar_shape = shape((8, LANES), F32)
    region = shape((cells, width), F32)
    field = pltpu.VMEM((rows, soundings, LANES), F32)
    same_core = [[CORES * peer + core for peer in range(peers)] for core in range(CORES)]
    swapped = [(device, device ^ 1) for device in range(orbits)]

    def exchange(array):
        flat = array.reshape(peers, 1, array.shape[0] // peers * LANES)
        flat = lax.all_to_all(
            flat, "orb", split_axis=0, concat_axis=0, axis_index_groups=same_core, tiled=True
        )
        return flat.reshape(array.shape)

    def swap(array):
        return lax.ppermute(array, "orb", swapped)

    in_hbm = [
        pltpu.with_memory_space_constraint(array, pltpu.HBM)
        for array in (block_rows, block_cells, observed, weights, footprint)
    ]
    outgoing, meta, packed_weights, footprint = call(
        functools.partial(start_kernel, cells),
        [
            delivered,
            pltpu.SMEM((3 * blocks,), jnp.int32),
            packed_shape,
            pltpu.VMEM(footprint.shape, F32),
        ],
        "hhhhh",
        "vsvv",
        [
            pltpu.VMEM(footprint.shape, footprint.dtype),
            field,
            pltpu.SMEM((peers,), jnp.int32),
            pltpu.SMEM((blocks,), jnp.int32),
            pltpu.SMEM((blocks,), jnp.int32),
            pltpu.VMEM(observed.shape, F32),
            pltpu.VMEM(weights.shape, F32),
            pltpu.SemaphoreType.DMA((4,)),
            pltpu.SemaphoreType.DMA((12,)),
        ],
    )(*in_hbm)
    half, collect, pick = call(
        first_gather_kernel,
        [
            shape((cells + own, width), F32),
            shape((cells, 3 * CAP * peers), BF16),
            shape((CAP * peers, 4 * cells), BF16),
        ],
        "vv",
    )(exchange(outgoing), precision_prior)
    prior, residual, sums, outgoing = call(
        first_update_kernel, [region, region, scalar_shape, fetched], "vvv"
    )(half, swap(half), pick)
    state, history, images = None, (), ()
    for iteration in range(ITERS):
        first, last = iteration == 0, iteration == ITERS - 1
        (partial,) = call(
            forward_kernel, [shape((reps, 24, LANES), F32)], "svvv", scratch=[field]
        )(meta, exchange(outgoing), sums, footprint)
        partial = lax.all_to_all(partial, "rep", split_axis=0, concat_axis=0, tiled=True)
        operands = [meta, partial, packed_weights, footprint]
        operands += [] if first else [state, *images]
        outgoing, *images = call(
            functools.partial(adjoint_kernel, iteration, last),
            [delivered] + ([] if last else [packed_shape] * (1 if first else 2)),
            "s" + "v" * (len(operands) - 1),
            scratch=[field],
        )(*operands)
        (half,) = call(gather_kernel, [shape((cells + 8, width), F32)], "vv")(
            exchange(outgoing), collect
        )
        operands = [half, swap(half), pick, prior, residual]
        operands += [] if first else [state, *history]
        results = call(
            functools.partial(update_kernel, first, last),
            [shape((own, width), F32)] * 2
            if last
            else [region, scalar_shape, fetched, scalar_shape, region, region, region],
            "v" * len(operands),
        )(*operands)
        if not last:
            residual, sums, outgoing, state, *history = results
    return tuple(results)


def solution(mesh):
    in_specs = (
        P("orb", None),
        P("orb", None),
        P("orb", "rep"),
        P("orb", None, "rep"),
        P("orb"),
        P("orb"),
    )
    out_specs = (P("orb", "rep"), P("orb", "rep"))
    return jax.shard_map(
        per_device, mesh=mesh, in_specs=in_specs, out_specs=out_specs, check_vma=False
    )
```

```python
import functools

import jax
import jax.numpy as jnp
from jax import lax
from jax.experimental import pallas as pl
from jax.experimental.pallas import tpu as pltpu
from jax.sharding import PartitionSpec as P

ITERS = 4
CORES = 2
CAP = 2 * CORES
FETCH = 2 * CAP
DELIVER = FETCH + 1
LANES = 128
SUB = 16
IN_FLIGHT = 6
F32 = jnp.float32
BF16 = jnp.bfloat16


def lane_ids(shape):
    return lax.broadcasted_iota(jnp.int32, shape, len(shape) - 1)


def three_parts(values):
    high = values.astype(BF16)
    rest = values - high.astype(F32)
    middle = rest.astype(BF16)
    low = (rest - middle.astype(F32)).astype(BF16)
    return high, middle, low


def spread(packed, field_ref):
    rows, soundings, _ = field_ref.shape
    for group in range(soundings // 8):
        for row in range(rows):
            lane = rows * group + row
            field_ref[row, 8 * group : 8 * group + 8, :] = jnp.broadcast_to(
                packed[:, lane : lane + 1], (8, LANES)
            )


def transposed_product(footprint_ref, field_ref, out_ref, block, row, place, keep_ref=None):
    soundings = footprint_ref.shape[1]
    left = jnp.zeros((SUB, LANES), F32)
    right = jnp.zeros((SUB, LANES), F32)
    for start in range(0, soundings, SUB):
        part = footprint_ref[block, start : start + SUB, :].astype(F32)
        if keep_ref is not None:
            keep_ref[block, start : start + SUB, :] = part
        z = field_ref[row, start : start + SUB, :]
        left = left + part[:, :LANES] * z
        right = right + part[:, LANES:] * z
    out_ref[pl.ds(place, 1), :] = jnp.sum(left, axis=0, keepdims=True)
    out_ref[pl.ds(place + 1, 1), :] = jnp.sum(right, axis=0, keepdims=True)


def each(first, last, together, do):
    def body(step, carry):
        for at in range(together):
            do(first + step * together + at)
        return carry

    lax.fori_loop(0, (last - first) // together, body, 0)


def in_columns(values):
    rows, soundings = values.shape
    parts = []
    for start in range(0, soundings, LANES):
        part = values[:, start : start + LANES]
        parts.append(jnp.concatenate([part] * (LANES // rows), axis=0).T)
    return jnp.concatenate(parts, axis=0)


def start_kernel(
    cells, rows_hbm, cells_hbm, observed_hbm, weights_hbm, prior_hbm, footprint_hbm,
    out_ref, meta_ref, packed_ref, prior_ref, footprint_ref,
    arrived_ref, field_ref, count_ref, rows_ref, cells_ref, observed_ref, weights_ref, sems, chunk_sems
):
    blocks = footprint_ref.shape[0]
    rows, soundings = weights_ref.shape
    peers = out_ref.shape[0] // DELIVER
    chunks = chunk_sems.shape[0]
    size = blocks // chunks
    small = [
        pltpu.make_async_copy(source, target, sems.at[at])
        for at, (source, target) in enumerate(
            [
                (rows_hbm, rows_ref),
                (cells_hbm, cells_ref),
                (observed_hbm, observed_ref),
                (weights_hbm, weights_ref),
                (prior_hbm, prior_ref),
            ]
        )
    ]
    for copy in small:
        copy.start()
    large = []
    for chunk in range(chunks):
        span = pl.ds(chunk * size, size)
        large.append(
            pltpu.make_async_copy(footprint_hbm.at[span], arrived_ref.at[span], chunk_sems.at[chunk])
        )
    for copy in large[:IN_FLIGHT]:
        copy.start()
    out_ref[...] = jnp.zeros_like(out_ref)
    for peer in range(peers):
        count_ref[peer] = 0
    for copy in small[:-1]:
        copy.wait()
    weights = weights_ref[...]
    columns = in_columns(weights * observed_ref[...])
    for row in range(rows):
        field_ref[row] = jnp.broadcast_to(columns[:, row : row + 1], (soundings, LANES))
    columns = in_columns(weights)
    groups = LANES // rows
    lanes = lane_ids((8, LANES)) // rows
    for half in range(soundings // LANES):
        packed = jnp.zeros((8, LANES), F32)
        for at in range(groups):
            start = half * LANES + 8 * at
            packed = jnp.where(lanes == at, columns[start : start + 8, :], packed)
        packed_ref[:, half * LANES : (half + 1) * LANES] = packed

    def product(block):
        cell = cells_ref[block]
        peer = cell // cells
        slot = cell % cells
        rank = count_ref[peer]
        count_ref[peer] = rank + 1
        row = rows_ref[block] % rows
        place = peer * DELIVER + 2 * rank
        meta_ref[block] = place
        meta_ref[blocks + block] = row
        meta_ref[2 * blocks + block] = peer * FETCH + 2 * rank
        scalars = pl.ds(peer * DELIVER + FETCH, 1)
        out_ref[scalars, :] = jnp.where(
            lane_ids((1, LANES)) == rank, (slot + 1).astype(F32), out_ref[scalars, :]
        )
        transposed_product(arrived_ref, field_ref, out_ref, block, row, place, footprint_ref)

    for chunk in range(chunks):
        large[chunk].wait()
        if chunk + IN_FLIGHT < chunks:
            large[chunk + IN_FLIGHT].start()
        each(chunk * size, (chunk + 1) * size, 4, product)
    small[-1].wait()


def serve(residual, pick, out_ref):
    peers = out_ref.shape[0] // FETCH
    high, middle, low = three_parts(residual)
    stacked = jnp.concatenate([high, middle, low, jnp.zeros_like(high)], axis=0)
    pieces = jnp.dot(pick, stacked, preferred_element_type=F32)
    for slot in range(CAP):
        for half in range(2):
            out_ref[pl.ds(2 * slot + half, peers, stride=FETCH), :] = pieces[
                slot * peers : (slot + 1) * peers, half * LANES : (half + 1) * LANES
            ]


def gathered(in_ref, collect):
    peers = in_ref.shape[0] // DELIVER
    slots = [
        jnp.concatenate(
            [in_ref[pl.ds(2 * slot + half, peers, stride=DELIVER), :] for half in range(2)], axis=1
        )
        for slot in range(CAP)
    ]
    high, middle, low = three_parts(jnp.concatenate(slots, axis=0))
    return jnp.dot(collect, jnp.concatenate([high, middle, low], axis=0), preferred_element_type=F32)


def arrived_scalars(in_ref):
    peers = in_ref.shape[0] // DELIVER
    row = jnp.sum(in_ref[pl.ds(FETCH, peers, stride=DELIVER), :], axis=0, keepdims=True)
    return jnp.broadcast_to(row, (8, LANES))


def everywhere(values, lane):
    return jnp.broadcast_to(values[:, lane : lane + 1], (8, LANES))


def spanning(tile, shape):
    rows, columns = shape
    return jnp.concatenate([jnp.concatenate([tile] * (columns // LANES), axis=1)] * (rows // 8), axis=0)


def lane_sums(values):
    tiles = [
        values[row : row + 8, column : column + LANES]
        for row in range(0, values.shape[0], 8)
        for column in range(0, values.shape[1], LANES)
    ]
    while len(tiles) > 1:
        tiles = [sum(tiles[at : at + 2]) for at in range(0, len(tiles), 2)]
    return jnp.broadcast_to(jnp.sum(tiles[0], axis=1, keepdims=True), (8, LANES))


def in_lanes(sums, first=0):
    lanes = lane_ids((8, LANES))
    packed = jnp.zeros((8, LANES), F32)
    for lane, value in enumerate(sums, first):
        packed = jnp.where(lanes == lane, value, packed)
    return packed


def first_gather_kernel(in_ref, prior_ref, half_ref, collect_ref, pick_ref):
    peers = in_ref.shape[0] // DELIVER
    own, width = prior_ref.shape
    cells = CORES * own
    ids = in_ref[pl.ds(FETCH, peers, stride=DELIVER), :]
    lanes = lane_ids((peers, LANES)).astype(F32)
    pick = jnp.concatenate(
        [(ids[:, slot : slot + 1] == lanes + 1.0).astype(F32) for slot in range(CAP)], axis=0
    )
    pick = jnp.where(lane_ids(pick.shape) < cells, pick, 0.0)
    collect = jnp.concatenate([pick.T[:cells, :]] * 3, axis=1).astype(BF16)
    collect_ref[...] = collect
    folds = [pick[:, :cells]] * 3 + [jnp.zeros((pick.shape[0], cells), F32)]
    pick_ref[...] = jnp.concatenate(folds, axis=1).astype(BF16)
    half_ref[0:cells, :] = gathered(in_ref, collect)
    half_ref[cells : cells + own, :] = prior_ref[...]


def gather_kernel(in_ref, collect_ref, half_ref):
    cells = collect_ref.shape[0]
    half_ref[0:cells, :] = gathered(in_ref, collect_ref[...])
    scalars = arrived_scalars(in_ref)
    half_ref[cells : cells + 8, :] = jnp.concatenate([scalars, jnp.zeros_like(scalars)], axis=1)


def partial_sums(prior, residual, direction=None):
    halved = 0.5 * residual
    weighted = prior * halved
    values = [halved * residual, weighted * residual]
    if direction is not None:
        values.append(weighted * direction)
    return in_lanes([lane_sums(value) for value in values])


def first_update_kernel(mine_ref, other_ref, pick_ref, prior_ref, residual_ref, sums_ref, out_ref):
    cells = residual_ref.shape[0]
    own = cells // CORES
    first = lax.axis_index("orb") % CORES == 0
    mine = mine_ref[cells : cells + own, :]
    other = other_ref[cells : cells + own, :]
    prior = jnp.concatenate([jnp.where(first, mine, other), jnp.where(first, other, mine)], axis=0)
    prior_ref[...] = prior
    residual = mine_ref[0:cells, :] + other_ref[0:cells, :]
    residual_ref[...] = residual
    sums_ref[...] = partial_sums(prior, residual)
    serve(residual, pick_ref[...], out_ref)


def update_kernel(first, last, *refs):
    mine_ref, other_ref, pick_ref, prior_ref, residual_ref, *refs = refs
    if not first:
        state_ref, direction_ref, image_ref, solution_ref, *refs = refs
    cells, width = residual_ref.shape
    sums = mine_ref[cells : cells + 8, :LANES] + other_ref[cells : cells + 8, :LANES]
    norm, prior_rr, prior_rd, forward_rr, forward_rd = [everywhere(sums, at) for at in range(5)]
    prior = prior_ref[...]
    residual = residual_ref[...]
    image = mine_ref[0:cells, :] + other_ref[0:cells, :] + prior * residual
    direction, prior_dd, forward_dd = residual, prior_rr, forward_rr
    if not first:
        beta = norm / state_ref[0:8, :]
        prior_dd = prior_rr + beta * (2.0 * prior_rd + beta * state_ref[8:16, :])
        forward_dd = forward_rr + beta * (2.0 * forward_rd + beta * state_ref[16:24, :])
        wide = spanning(beta, (cells, width))
        direction = residual + wide * direction_ref[...]
        image = image + wide * image_ref[...]
    alpha = spanning(norm / (prior_dd + forward_dd), (cells, width))
    new_residual = residual - alpha * image
    solution = alpha * direction if first else solution_ref[...] + alpha * direction
    if last:
        new_solution_ref, new_residual_ref = refs
        own = cells // CORES
        core_first = lax.axis_index("orb") % CORES == 0
        new_solution_ref[...] = jnp.where(core_first, solution[:own], solution[own:])
        new_residual_ref[...] = jnp.where(core_first, new_residual[:own], new_residual[own:])
        return
    new_residual_ref, sums_ref, out_ref, new_state_ref, new_direction_ref, new_image_ref, new_solution_ref = refs
    serve(new_residual, pick_ref[...], out_ref)
    sums_ref[...] = partial_sums(prior, new_residual, direction)
    new_residual_ref[...] = new_residual
    new_state_ref[0:8, :] = norm
    new_state_ref[8:16, :] = prior_dd
    new_state_ref[16:24, :] = forward_dd
    new_state_ref[24:32, :] = jnp.zeros_like(norm) if first else beta
    new_direction_ref[...] = direction
    new_image_ref[...] = image
    new_solution_ref[...] = solution


def forward_kernel(meta_ref, in_ref, scalars_ref, footprint_ref, out_ref, sums_ref):
    blocks = footprint_ref.shape[0]
    rows, soundings, _ = sums_ref.shape
    sums_ref[...] = jnp.zeros_like(sums_ref)

    def product(block):
        row = meta_ref[blocks + block]
        place = meta_ref[2 * blocks + block]
        left = jnp.broadcast_to(in_ref[pl.ds(place, 1), :], (2 * SUB, LANES))
        right = jnp.broadcast_to(in_ref[pl.ds(place + 1, 1), :], (2 * SUB, LANES))
        for start in range(0, soundings, 2 * SUB):
            part = footprint_ref[block, start : start + 2 * SUB, :]
            sums_ref[row, start : start + 2 * SUB, :] += part[:, :LANES] * left + part[:, LANES:] * right

    each(0, blocks, 4, product)
    lanes = lane_ids((8, LANES))
    per_half = LANES // rows
    halves = []
    for half in range(soundings // 8 // per_half):
        packed = [jnp.zeros((8, LANES), F32) for _ in range(4)]
        for at in range(per_half):
            group = half * per_half + at
            for row in range(rows):
                summed = jnp.sum(sums_ref[row, 8 * group : 8 * group + 8, :], axis=1, keepdims=True)
                packed[row % 4] = jnp.where(lanes == rows * at + row, summed, packed[row % 4])
        halves.append((packed[0] + packed[1]) + (packed[2] + packed[3]))
    halves.append(scalars_ref[...])
    message = jnp.concatenate(halves, axis=0)
    for peer in range(out_ref.shape[0]):
        out_ref[peer] = message


def adjoint_kernel(iteration, last, *refs):
    meta_ref, in_ref, weights_ref, footprint_ref, *refs = refs
    if iteration > 0:
        state_ref, old_ref, *refs = refs
    if iteration > 1:
        older_ref, *refs = refs
    out_ref, *refs = refs
    blocks = footprint_ref.shape[0]
    peers = out_ref.shape[0] // DELIVER
    summed = in_ref[0]
    for peer in range(1, in_ref.shape[0]):
        summed = summed + in_ref[peer]
    forward = jnp.concatenate([summed[0:8], summed[8:16]], axis=1)
    field = weights_ref[...] * forward
    *refs, field_ref = refs
    out_ref[...] = jnp.zeros_like(out_ref)
    spread(field, field_ref)
    sums = [lane_sums(field * forward)]
    if iteration > 0:
        direction = old_ref[...]
        if iteration > 1:
            direction = direction + spanning(state_ref[24:32, :], direction.shape) * older_ref[...]
        sums.append(lane_sums(field * direction))
    if not last:
        refs[0][...] = forward
        if iteration > 0:
            refs[1][...] = direction
    scalars = jnp.sum(summed[16:24] + in_lanes(sums, 3), axis=0, keepdims=True)
    out_ref[pl.ds(FETCH, peers, stride=DELIVER), :] = jnp.broadcast_to(scalars, (peers, LANES))

    def product(block):
        transposed_product(
            footprint_ref, field_ref, out_ref, block, meta_ref[blocks + block], meta_ref[block]
        )

    each(0, blocks, 8, product)


def call(kernel, out_shape, kinds, out_kinds=None, scratch=()):
    spaces = {"v": pltpu.VMEM, "s": pltpu.SMEM, "h": pl.ANY}
    out_kinds = out_kinds or "v" * len(out_shape)
    return pl.pallas_call(
        kernel,
        out_shape=out_shape,
        in_specs=[pl.BlockSpec(memory_space=spaces[kind]) for kind in kinds],
        out_specs=[pl.BlockSpec(memory_space=spaces[kind]) for kind in out_kinds],
        scratch_shapes=list(scratch),
        compiler_params=pltpu.CompilerParams(vmem_limit_bytes=16 * 1024 * 1024),
    )


def per_device(observed, weights, precision_prior, footprint, block_rows, block_cells):
    rows, soundings = observed.shape
    own, width = precision_prior.shape
    cells = CORES * own
    blocks = footprint.shape[0]
    orbits = lax.axis_size("orb")
    reps = lax.axis_size("rep")
    peers = orbits // CORES
    shape = jax.ShapeDtypeStruct
    fetched = shape((peers * FETCH, LANES), F32)
    delivered = shape((peers * DELIVER, LANES), F32)
    packed_shape = shape((8, soundings * rows // 8), F32)
    scalar_shape = shape((8, LANES), F32)
    state_shape = shape((32, LANES), F32)
    region = shape((cells, width), F32)
    field = pltpu.VMEM((rows, soundings, LANES), F32)
    same_core = [[CORES * peer + core for peer in range(peers)] for core in range(CORES)]
    swapped = [(device, device ^ 1) for device in range(orbits)]

    def exchange(array):
        flat = array.reshape(peers, 1, array.shape[0] // peers * LANES)
        flat = lax.all_to_all(
            flat, "orb", split_axis=0, concat_axis=0, axis_index_groups=same_core, tiled=True
        )
        return flat.reshape(array.shape)

    def swap(array):
        return lax.ppermute(array, "orb", swapped)

    in_hbm = [
        pltpu.with_memory_space_constraint(array, pltpu.HBM)
        for array in (block_rows, block_cells, observed, weights, precision_prior, footprint)
    ]
    outgoing, meta, packed_weights, own_prior, footprint = call(
        functools.partial(start_kernel, cells),
        [
            delivered,
            pltpu.SMEM((3 * blocks,), jnp.int32),
            packed_shape,
            pltpu.VMEM(precision_prior.shape, F32),
            pltpu.VMEM(footprint.shape, F32),
        ],
        "hhhhhh",
        "vsvvv",
        [
            pltpu.VMEM(footprint.shape, footprint.dtype),
            field,
            pltpu.SMEM((peers,), jnp.int32),
            pltpu.SMEM((blocks,), jnp.int32),
            pltpu.SMEM((blocks,), jnp.int32),
            pltpu.VMEM(observed.shape, F32),
            pltpu.VMEM(weights.shape, F32),
            pltpu.SemaphoreType.DMA((5,)),
            pltpu.SemaphoreType.DMA((12,)),
        ],
    )(*in_hbm)
    half, collect, pick = call(
        first_gather_kernel,
        [
            shape((cells + own, width), F32),
            shape((cells, 3 * CAP * peers), BF16),
            shape((CAP * peers, 4 * cells), BF16),
        ],
        "vv",
    )(exchange(outgoing), own_prior)
    prior, residual, sums, outgoing = call(
        first_update_kernel, [region, region, scalar_shape, fetched], "vvv"
    )(half, swap(half), pick)
    state, history, images = None, (), ()
    for iteration in range(ITERS):
        first, last = iteration == 0, iteration == ITERS - 1
        (partial,) = call(
            forward_kernel, [shape((reps, 24, LANES), F32)], "svvv", scratch=[field]
        )(meta, exchange(outgoing), sums, footprint)
        partial = lax.all_to_all(partial, "rep", split_axis=0, concat_axis=0, tiled=True)
        operands = [meta, partial, packed_weights, footprint]
        operands += [] if first else [state, *images]
        outgoing, *images = call(
            functools.partial(adjoint_kernel, iteration, last),
            [delivered] + ([] if last else [packed_shape] * (1 if first else 2)),
            "s" + "v" * (len(operands) - 1),
            scratch=[field],
        )(*operands)
        (half,) = call(gather_kernel, [shape((cells + 8, width), F32)], "vv")(
            exchange(outgoing), collect
        )
        operands = [half, swap(half), pick, prior, residual]
        operands += [] if first else [state, *history]
        results = call(
            functools.partial(update_kernel, first, last),
            [shape((own, width), F32)] * 2
            if last
            else [region, scalar_shape, fetched, state_shape, region, region, region],
            "v" * len(operands),
        )(*operands)
        if not last:
            residual, sums, outgoing, state, *history = results
    return tuple(results)


def solution(mesh):
    in_specs = (
        P("orb", None),
        P("orb", None),
        P("orb", "rep"),
        P("orb", None, "rep"),
        P("orb"),
        P("orb"),
    )
    out_specs = (P("orb", "rep"), P("orb", "rep"))
    return jax.shard_map(
        per_device, mesh=mesh, in_specs=in_specs, out_specs=out_specs, check_vma=False
    )
```

```python
import functools

import jax
import jax.numpy as jnp
from jax import lax
from jax.experimental import pallas as pl
from jax.experimental.pallas import tpu as pltpu
from jax.sharding import PartitionSpec as P

ITERS = 4
CORES = 2
CAP = 2 * CORES
FETCH = 2 * CAP
DELIVER = FETCH + 1
LANES = 128
SUB = 16
IN_FLIGHT = 6
F32 = jnp.float32
BF16 = jnp.bfloat16


def lane_ids(shape):
    return lax.broadcasted_iota(jnp.int32, shape, len(shape) - 1)


def three_parts(values):
    high = values.astype(BF16)
    rest = values - high.astype(F32)
    middle = rest.astype(BF16)
    low = (rest - middle.astype(F32)).astype(BF16)
    return high, middle, low


def spread(packed, field_ref):
    rows, soundings, _ = field_ref.shape
    for group in range(soundings // 8):
        for row in range(rows):
            lane = rows * group + row
            field_ref[row, 8 * group : 8 * group + 8, :] = jnp.broadcast_to(
                packed[:, lane : lane + 1], (8, LANES)
            )


def transposed_product(footprint_ref, field_ref, out_ref, block, row, place, keep_ref=None):
    soundings = footprint_ref.shape[1]
    left = jnp.zeros((SUB, LANES), F32)
    right = jnp.zeros((SUB, LANES), F32)
    for start in range(0, soundings, SUB):
        part = footprint_ref[block, start : start + SUB, :].astype(F32)
        if keep_ref is not None:
            keep_ref[block, start : start + SUB, :] = part
        z = field_ref[row, start : start + SUB, :]
        left = left + part[:, :LANES] * z
        right = right + part[:, LANES:] * z
    out_ref[pl.ds(place, 1), :] = jnp.sum(left, axis=0, keepdims=True)
    out_ref[pl.ds(place + 1, 1), :] = jnp.sum(right, axis=0, keepdims=True)


def each(first, last, together, do):
    def body(step, carry):
        for at in range(together):
            do(first + step * together + at)
        return carry

    lax.fori_loop(0, (last - first) // together, body, 0)


def in_columns(values):
    rows, soundings = values.shape
    parts = []
    for start in range(0, soundings, LANES):
        part = values[:, start : start + LANES]
        parts.append(jnp.concatenate([part] * (LANES // rows), axis=0).T)
    return jnp.concatenate(parts, axis=0)


def start_kernel(
    cells, rows_hbm, cells_hbm, observed_hbm, weights_hbm, prior_hbm, footprint_hbm,
    out_ref, meta_ref, packed_ref, prior_ref, footprint_ref,
    arrived_ref, field_ref, count_ref, rows_ref, cells_ref, observed_ref, weights_ref, sems, chunk_sems
):
    blocks = footprint_ref.shape[0]
    rows, soundings = weights_ref.shape
    peers = out_ref.shape[0] // DELIVER
    chunks = chunk_sems.shape[0]
    size = blocks // chunks
    small = [
        pltpu.make_async_copy(source, target, sems.at[at])
        for at, (source, target) in enumerate(
            [
                (rows_hbm, rows_ref),
                (cells_hbm, cells_ref),
                (observed_hbm, observed_ref),
                (weights_hbm, weights_ref),
                (prior_hbm, prior_ref),
            ]
        )
    ]
    for copy in small:
        copy.start()
    large = []
    for chunk in range(chunks):
        span = pl.ds(chunk * size, size)
        large.append(
            pltpu.make_async_copy(footprint_hbm.at[span], arrived_ref.at[span], chunk_sems.at[chunk])
        )
    for copy in large[:IN_FLIGHT]:
        copy.start()
    out_ref[...] = jnp.zeros_like(out_ref)
    for peer in range(peers):
        count_ref[peer] = 0
    for copy in small[:-1]:
        copy.wait()
    weights = weights_ref[...]
    columns = in_columns(weights * observed_ref[...])
    for row in range(rows):
        field_ref[row] = jnp.broadcast_to(columns[:, row : row + 1], (soundings, LANES))
    columns = in_columns(weights)
    groups = LANES // rows
    lanes = lane_ids((8, LANES)) // rows
    for half in range(soundings // LANES):
        packed = jnp.zeros((8, LANES), F32)
        for at in range(groups):
            start = half * LANES + 8 * at
            packed = jnp.where(lanes == at, columns[start : start + 8, :], packed)
        packed_ref[:, half * LANES : (half + 1) * LANES] = packed

    def product(block):
        cell = cells_ref[block]
        peer = cell // cells
        slot = cell % cells
        rank = count_ref[peer]
        count_ref[peer] = rank + 1
        row = rows_ref[block] % rows
        place = peer * DELIVER + 2 * rank
        meta_ref[block] = place
        meta_ref[blocks + block] = row
        meta_ref[2 * blocks + block] = peer * FETCH + 2 * rank
        scalars = pl.ds(peer * DELIVER + FETCH, 1)
        out_ref[scalars, :] = jnp.where(
            lane_ids((1, LANES)) == rank, (slot + 1).astype(F32), out_ref[scalars, :]
        )
        transposed_product(arrived_ref, field_ref, out_ref, block, row, place, footprint_ref)

    for chunk in range(chunks):
        large[chunk].wait()
        if chunk + IN_FLIGHT < chunks:
            large[chunk + IN_FLIGHT].start()
        each(chunk * size, (chunk + 1) * size, 4, product)
    small[-1].wait()


def serve(residual, pick, out_ref):
    peers = out_ref.shape[0] // FETCH
    high, middle, low = three_parts(residual)
    stacked = jnp.concatenate([high, middle, low, jnp.zeros_like(high)], axis=0)
    pieces = jnp.dot(pick, stacked, preferred_element_type=F32)
    for slot in range(CAP):
        for half in range(2):
            out_ref[pl.ds(2 * slot + half, peers, stride=FETCH), :] = pieces[
                slot * peers : (slot + 1) * peers, half * LANES : (half + 1) * LANES
            ]


def gathered(in_ref, collect):
    peers = in_ref.shape[0] // DELIVER
    slots = [
        jnp.concatenate(
            [in_ref[pl.ds(2 * slot + half, peers, stride=DELIVER), :] for half in range(2)], axis=1
        )
        for slot in range(CAP)
    ]
    high, middle, low = three_parts(jnp.concatenate(slots, axis=0))
    return jnp.dot(collect, jnp.concatenate([high, middle, low], axis=0), preferred_element_type=F32)


def arrived_scalars(in_ref):
    peers = in_ref.shape[0] // DELIVER
    row = jnp.sum(in_ref[pl.ds(FETCH, peers, stride=DELIVER), :], axis=0, keepdims=True)
    return jnp.broadcast_to(row, (8, LANES))


def everywhere(values, lane):
    return jnp.broadcast_to(values[:, lane : lane + 1], (8, LANES))


def spanning(tile, shape):
    rows, columns = shape
    return jnp.concatenate([jnp.concatenate([tile] * (columns // LANES), axis=1)] * (rows // 8), axis=0)


def lane_sums(values):
    tiles = [
        values[row : row + 8, column : column + LANES]
        for row in range(0, values.shape[0], 8)
        for column in range(0, values.shape[1], LANES)
    ]
    while len(tiles) > 1:
        tiles = [sum(tiles[at : at + 2]) for at in range(0, len(tiles), 2)]
    return jnp.broadcast_to(jnp.sum(tiles[0], axis=1, keepdims=True), (8, LANES))


def in_lanes(sums, first=0):
    lanes = lane_ids((8, LANES))
    packed = jnp.zeros((8, LANES), F32)
    for lane, value in enumerate(sums, first):
        packed = jnp.where(lanes == lane, value, packed)
    return packed


def first_gather_kernel(in_ref, prior_ref, half_ref, collect_ref, pick_ref):
    peers = in_ref.shape[0] // DELIVER
    own, width = prior_ref.shape
    cells = CORES * own
    ids = in_ref[pl.ds(FETCH, peers, stride=DELIVER), :]
    lanes = lane_ids((peers, LANES)).astype(F32)
    pick = jnp.concatenate(
        [(ids[:, slot : slot + 1] == lanes + 1.0).astype(F32) for slot in range(CAP)], axis=0
    )
    pick = jnp.where(lane_ids(pick.shape) < cells, pick, 0.0)
    collect = jnp.concatenate([pick.T[:cells, :]] * 3, axis=1).astype(BF16)
    collect_ref[...] = collect
    folds = [pick[:, :cells]] * 3 + [jnp.zeros((pick.shape[0], cells), F32)]
    pick_ref[...] = jnp.concatenate(folds, axis=1).astype(BF16)
    half_ref[0:cells, :] = gathered(in_ref, collect)
    half_ref[cells : cells + own, :] = prior_ref[...]


def gather_kernel(in_ref, collect_ref, half_ref):
    cells = collect_ref.shape[0]
    half_ref[0:cells, :] = gathered(in_ref, collect_ref[...])
    scalars = arrived_scalars(in_ref)
    half_ref[cells : cells + 8, :] = jnp.concatenate([scalars, jnp.zeros_like(scalars)], axis=1)


def partial_sums(prior, residual, direction=None):
    halved = 0.5 * residual
    weighted = prior * halved
    values = [halved * residual, weighted * residual]
    if direction is not None:
        values.append(weighted * direction)
    return in_lanes([lane_sums(value) for value in values])


def first_update_kernel(mine_ref, other_ref, pick_ref, prior_ref, residual_ref, sums_ref, out_ref):
    cells = residual_ref.shape[0]
    own = cells // CORES
    first = lax.axis_index("orb") % CORES == 0
    mine = mine_ref[cells : cells + own, :]
    other = other_ref[cells : cells + own, :]
    prior = jnp.concatenate([jnp.where(first, mine, other), jnp.where(first, other, mine)], axis=0)
    prior_ref[...] = prior
    residual = mine_ref[0:cells, :] + other_ref[0:cells, :]
    residual_ref[...] = residual
    sums_ref[...] = partial_sums(prior, residual)
    serve(residual, pick_ref[...], out_ref)


def update_kernel(first, last, *refs):
    mine_ref, other_ref, pick_ref, prior_ref, residual_ref, *refs = refs
    if not first:
        state_ref, direction_ref, image_ref, solution_ref, *refs = refs
    cells, width = residual_ref.shape
    sums = mine_ref[cells : cells + 8, :LANES] + other_ref[cells : cells + 8, :LANES]
    norm, prior_rr, prior_rd, forward_rr, forward_rd = [everywhere(sums, at) for at in range(5)]
    prior = prior_ref[...]
    residual = residual_ref[...]
    image = mine_ref[0:cells, :] + other_ref[0:cells, :] + prior * residual
    direction, prior_dd, forward_dd = residual, prior_rr, forward_rr
    if not first:
        beta = norm / state_ref[0:8, :]
        prior_dd = prior_rr + beta * (2.0 * prior_rd + beta * state_ref[8:16, :])
        forward_dd = forward_rr + beta * (2.0 * forward_rd + beta * state_ref[16:24, :])
        wide = spanning(beta, (cells, width))
        direction = residual + wide * direction_ref[...]
        image = image + wide * image_ref[...]
    alpha = spanning(norm / (prior_dd + forward_dd), (cells, width))
    new_residual = residual - alpha * image
    solution = alpha * direction if first else solution_ref[...] + alpha * direction
    if last:
        new_solution_ref, new_residual_ref = refs
        own = cells // CORES
        core_first = lax.axis_index("orb") % CORES == 0
        new_solution_ref[...] = jnp.where(core_first, solution[:own], solution[own:])
        new_residual_ref[...] = jnp.where(core_first, new_residual[:own], new_residual[own:])
        return
    new_residual_ref, sums_ref, out_ref, new_state_ref, new_direction_ref, new_image_ref, new_solution_ref = refs
    serve(new_residual, pick_ref[...], out_ref)
    sums_ref[...] = partial_sums(prior, new_residual, direction)
    new_residual_ref[...] = new_residual
    new_state_ref[0:8, :] = norm
    new_state_ref[8:16, :] = prior_dd
    new_state_ref[16:24, :] = forward_dd
    new_state_ref[24:32, :] = jnp.zeros_like(norm) if first else beta
    new_direction_ref[...] = direction
    new_image_ref[...] = image
    new_solution_ref[...] = solution


def forward_kernel(meta_ref, in_ref, scalars_ref, footprint_ref, out_ref, sums_ref):
    blocks = footprint_ref.shape[0]
    rows, soundings, _ = sums_ref.shape
    sums_ref[...] = jnp.zeros_like(sums_ref)

    def product(block):
        row = meta_ref[blocks + block]
        place = meta_ref[2 * blocks + block]
        left = jnp.broadcast_to(in_ref[pl.ds(place, 1), :], (2 * SUB, LANES))
        right = jnp.broadcast_to(in_ref[pl.ds(place + 1, 1), :], (2 * SUB, LANES))
        for start in range(0, soundings, 2 * SUB):
            part = footprint_ref[block, start : start + 2 * SUB, :]
            sums_ref[row, start : start + 2 * SUB, :] += part[:, :LANES] * left + part[:, LANES:] * right

    each(0, blocks, 4, product)
    lanes = lane_ids((8, LANES))
    per_half = LANES // rows
    halves = []
    for half in range(soundings // 8 // per_half):
        packed = [jnp.zeros((8, LANES), F32) for _ in range(4)]
        for at in range(per_half):
            group = half * per_half + at
            for row in range(rows):
                summed = jnp.sum(sums_ref[row, 8 * group : 8 * group + 8, :], axis=1, keepdims=True)
                packed[row % 4] = jnp.where(lanes == rows * at + row, summed, packed[row % 4])
        halves.append((packed[0] + packed[1]) + (packed[2] + packed[3]))
    halves.append(scalars_ref[...])
    out_ref[...] = jnp.concatenate(halves, axis=0)


def adjoint_kernel(iteration, last, *refs):
    meta_ref, own_ref, next_ref, previous_ref, opposite_ref, weights_ref, footprint_ref, *refs = refs
    if iteration > 0:
        state_ref, old_ref, *refs = refs
    if iteration > 1:
        older_ref, *refs = refs
    out_ref, *refs = refs
    blocks = footprint_ref.shape[0]
    peers = out_ref.shape[0] // DELIVER
    summed = (own_ref[...] + opposite_ref[...]) + (next_ref[...] + previous_ref[...])
    forward = jnp.concatenate([summed[0:8], summed[8:16]], axis=1)
    field = weights_ref[...] * forward
    *refs, field_ref = refs
    out_ref[...] = jnp.zeros_like(out_ref)
    spread(field, field_ref)
    sums = [lane_sums(field * forward)]
    if iteration > 0:
        direction = old_ref[...]
        if iteration > 1:
            direction = direction + spanning(state_ref[24:32, :], direction.shape) * older_ref[...]
        sums.append(lane_sums(field * direction))
    if not last:
        refs[0][...] = forward
        if iteration > 0:
            refs[1][...] = direction
    scalars = jnp.sum(summed[16:24] + in_lanes(sums, 3), axis=0, keepdims=True)
    out_ref[pl.ds(FETCH, peers, stride=DELIVER), :] = jnp.broadcast_to(scalars, (peers, LANES))

    def product(block):
        transposed_product(
            footprint_ref, field_ref, out_ref, block, meta_ref[blocks + block], meta_ref[block]
        )

    each(0, blocks, 8, product)


def call(kernel, out_shape, kinds, out_kinds=None, scratch=()):
    spaces = {"v": pltpu.VMEM, "s": pltpu.SMEM, "h": pl.ANY}
    out_kinds = out_kinds or "v" * len(out_shape)
    return pl.pallas_call(
        kernel,
        out_shape=out_shape,
        in_specs=[pl.BlockSpec(memory_space=spaces[kind]) for kind in kinds],
        out_specs=[pl.BlockSpec(memory_space=spaces[kind]) for kind in out_kinds],
        scratch_shapes=list(scratch),
        compiler_params=pltpu.CompilerParams(vmem_limit_bytes=16 * 1024 * 1024),
    )


def per_device(observed, weights, precision_prior, footprint, block_rows, block_cells):
    rows, soundings = observed.shape
    own, width = precision_prior.shape
    cells = CORES * own
    blocks = footprint.shape[0]
    orbits = lax.axis_size("orb")
    reps = lax.axis_size("rep")
    peers = orbits // CORES
    shape = jax.ShapeDtypeStruct
    fetched = shape((peers * FETCH, LANES), F32)
    delivered = shape((peers * DELIVER, LANES), F32)
    packed_shape = shape((8, soundings * rows // 8), F32)
    scalar_shape = shape((8, LANES), F32)
    state_shape = shape((32, LANES), F32)
    region = shape((cells, width), F32)
    field = pltpu.VMEM((rows, soundings, LANES), F32)
    same_core = [[CORES * peer + core for peer in range(peers)] for core in range(CORES)]
    swapped = [(device, device ^ 1) for device in range(orbits)]

    def exchange(array):
        flat = array.reshape(peers, 1, array.shape[0] // peers * LANES)
        flat = lax.all_to_all(
            flat, "orb", split_axis=0, concat_axis=0, axis_index_groups=same_core, tiled=True
        )
        return flat.reshape(array.shape)

    def swap(array):
        return lax.ppermute(array, "orb", swapped)

    in_hbm = [
        pltpu.with_memory_space_constraint(array, pltpu.HBM)
        for array in (block_rows, block_cells, observed, weights, precision_prior, footprint)
    ]
    outgoing, meta, packed_weights, own_prior, footprint = call(
        functools.partial(start_kernel, cells),
        [
            delivered,
            pltpu.SMEM((3 * blocks,), jnp.int32),
            packed_shape,
            pltpu.VMEM(precision_prior.shape, F32),
            pltpu.VMEM(footprint.shape, F32),
        ],
        "hhhhhh",
        "vsvvv",
        [
            pltpu.VMEM(footprint.shape, footprint.dtype),
            field,
            pltpu.SMEM((peers,), jnp.int32),
            pltpu.SMEM((blocks,), jnp.int32),
            pltpu.SMEM((blocks,), jnp.int32),
            pltpu.VMEM(observed.shape, F32),
            pltpu.VMEM(weights.shape, F32),
            pltpu.SemaphoreType.DMA((5,)),
            pltpu.SemaphoreType.DMA((12,)),
        ],
    )(*in_hbm)
    half, collect, pick = call(
        first_gather_kernel,
        [
            shape((cells + own, width), F32),
            shape((cells, 3 * CAP * peers), BF16),
            shape((CAP * peers, 4 * cells), BF16),
        ],
        "vv",
    )(exchange(outgoing), own_prior)
    prior, residual, sums, outgoing = call(
        first_update_kernel, [region, region, scalar_shape, fetched], "vvv"
    )(half, swap(half), pick)
    state, history, images = None, (), ()
    for iteration in range(ITERS):
        first, last = iteration == 0, iteration == ITERS - 1
        (partial,) = call(
            forward_kernel, [shape((24, LANES), F32)], "svvv", scratch=[field]
        )(meta, exchange(outgoing), sums, footprint)
        others = [
            lax.ppermute(partial, "rep", [(device, (device + by) % reps) for device in range(reps)])
            for by in (1, 3, 2)
        ]
        operands = [meta, partial, *others, packed_weights, footprint]
        operands += [] if first else [state, *images]
        outgoing, *images = call(
            functools.partial(adjoint_kernel, iteration, last),
            [delivered] + ([] if last else [packed_shape] * (1 if first else 2)),
            "s" + "v" * (len(operands) - 1),
            scratch=[field],
        )(*operands)
        (half,) = call(gather_kernel, [shape((cells + 8, width), F32)], "vv")(
            exchange(outgoing), collect
        )
        operands = [half, swap(half), pick, prior, residual]
        operands += [] if first else [state, *history]
        results = call(
            functools.partial(update_kernel, first, last),
            [shape((own, width), F32)] * 2
            if last
            else [region, scalar_shape, fetched, state_shape, region, region, region],
            "v" * len(operands),
        )(*operands)
        if not last:
            residual, sums, outgoing, state, *history = results
    return tuple(results)


def solution(mesh):
    in_specs = (
        P("orb", None),
        P("orb", None),
        P("orb", "rep"),
        P("orb", None, "rep"),
        P("orb"),
        P("orb"),
    )
    out_specs = (P("orb", "rep"), P("orb", "rep"))
    return jax.shard_map(
        per_device, mesh=mesh, in_specs=in_specs, out_specs=out_specs, check_vma=False
    )
```

```python
import functools

import jax
import jax.numpy as jnp
from jax import lax
from jax.experimental import pallas as pl
from jax.experimental.pallas import tpu as pltpu
from jax.sharding import PartitionSpec as P

ITERS = 4
CORES = 2
CAP = 2 * CORES
FETCH = 2 * CAP
DELIVER = FETCH + 1
LANES = 128
SUB = 16
IN_FLIGHT = 6
F32 = jnp.float32
BF16 = jnp.bfloat16


def lane_ids(shape):
    return lax.broadcasted_iota(jnp.int32, shape, len(shape) - 1)


def three_parts(values):
    high = values.astype(BF16)
    rest = values - high.astype(F32)
    middle = rest.astype(BF16)
    low = (rest - middle.astype(F32)).astype(BF16)
    return high, middle, low


def spread(packed, field_ref):
    rows, soundings, _ = field_ref.shape
    for group in range(soundings // 8):
        for row in range(rows):
            lane = rows * group + row
            field_ref[row, 8 * group : 8 * group + 8, :] = jnp.broadcast_to(
                packed[:, lane : lane + 1], (8, LANES)
            )


def transposed_product(footprint_ref, field_ref, out_ref, block, row, place, keep_ref=None):
    soundings = footprint_ref.shape[1]
    left = jnp.zeros((SUB, LANES), F32)
    right = jnp.zeros((SUB, LANES), F32)
    for start in range(0, soundings, SUB):
        part = footprint_ref[block, start : start + SUB, :].astype(F32)
        if keep_ref is not None:
            keep_ref[block, start : start + SUB, :] = part
        z = field_ref[row, start : start + SUB, :]
        left = left + part[:, :LANES] * z
        right = right + part[:, LANES:] * z
    out_ref[pl.ds(place, 1), :] = jnp.sum(left, axis=0, keepdims=True)
    out_ref[pl.ds(place + 1, 1), :] = jnp.sum(right, axis=0, keepdims=True)


def each(first, last, together, do):
    def body(step, carry):
        for at in range(together):
            do(first + step * together + at)
        return carry

    lax.fori_loop(0, (last - first) // together, body, 0)


def in_columns(values):
    rows, soundings = values.shape
    parts = []
    for start in range(0, soundings, LANES):
        part = values[:, start : start + LANES]
        parts.append(jnp.concatenate([part] * (LANES // rows), axis=0).T)
    return jnp.concatenate(parts, axis=0)


def start_kernel(
    cells, rows_hbm, cells_hbm, observed_hbm, weights_hbm, prior_hbm, footprint_hbm,
    out_ref, meta_ref, packed_ref, prior_ref, footprint_ref,
    arrived_ref, field_ref, count_ref, rows_ref, cells_ref, observed_ref, weights_ref, sems, chunk_sems
):
    blocks = footprint_ref.shape[0]
    rows, soundings = weights_ref.shape
    peers = out_ref.shape[0] // DELIVER
    chunks = chunk_sems.shape[0]
    shift = cells.bit_length() - 1
    assert cells == 1 << shift and rows & (rows - 1) == 0
    size = blocks // chunks
    small = [
        pltpu.make_async_copy(source, target, sems.at[at])
        for at, (source, target) in enumerate(
            [
                (rows_hbm, rows_ref),
                (cells_hbm, cells_ref),
                (observed_hbm, observed_ref),
                (weights_hbm, weights_ref),
                (prior_hbm, prior_ref),
            ]
        )
    ]
    for copy in small:
        copy.start()
    large = []
    for chunk in range(chunks):
        span = pl.ds(chunk * size, size)
        large.append(
            pltpu.make_async_copy(footprint_hbm.at[span], arrived_ref.at[span], chunk_sems.at[chunk])
        )
    for copy in large[:IN_FLIGHT]:
        copy.start()
    out_ref[...] = jnp.zeros_like(out_ref)
    for peer in range(peers):
        count_ref[peer] = 0
    for copy in small[:-1]:
        copy.wait()
    weights = weights_ref[...]
    columns = in_columns(weights * observed_ref[...])
    for row in range(rows):
        field_ref[row] = jnp.broadcast_to(columns[:, row : row + 1], (soundings, LANES))
    columns = in_columns(weights)
    groups = LANES // rows
    lanes = lane_ids((8, LANES)) // rows
    for half in range(soundings // LANES):
        packed = jnp.zeros((8, LANES), F32)
        for at in range(groups):
            start = half * LANES + 8 * at
            packed = jnp.where(lanes == at, columns[start : start + 8, :], packed)
        packed_ref[:, half * LANES : (half + 1) * LANES] = packed

    def product(block):
        cell = cells_ref[block]
        peer = lax.shift_right_logical(cell, shift)
        slot = cell & (cells - 1)
        rank = count_ref[peer]
        count_ref[peer] = rank + 1
        row = rows_ref[block] & (rows - 1)
        place = peer * DELIVER + 2 * rank
        meta_ref[block] = place
        meta_ref[blocks + block] = row
        meta_ref[2 * blocks + block] = peer * FETCH + 2 * rank
        pltpu.store(
            out_ref.at[pl.ds(peer * DELIVER + FETCH, 1), :],
            jnp.full((1, LANES), (slot + 1).astype(F32)),
            mask=lane_ids((1, LANES)) == rank,
        )
        transposed_product(arrived_ref, field_ref, out_ref, block, row, place, footprint_ref)

    for chunk in range(chunks):
        large[chunk].wait()
        if chunk + IN_FLIGHT < chunks:
            large[chunk + IN_FLIGHT].start()
        each(chunk * size, (chunk + 1) * size, 4, product)
    small[-1].wait()


def serve(residual, pick, out_ref):
    peers = out_ref.shape[0] // FETCH
    high, middle, low = three_parts(residual)
    stacked = jnp.concatenate([high, middle, low, jnp.zeros_like(high)], axis=0)
    pieces = jnp.dot(pick, stacked, preferred_element_type=F32)
    for slot in range(CAP):
        for half in range(2):
            out_ref[pl.ds(2 * slot + half, peers, stride=FETCH), :] = pieces[
                slot * peers : (slot + 1) * peers, half * LANES : (half + 1) * LANES
            ]


def gathered(in_ref, collect):
    peers = in_ref.shape[0] // DELIVER
    slots = [
        jnp.concatenate(
            [in_ref[pl.ds(2 * slot + half, peers, stride=DELIVER), :] for half in range(2)], axis=1
        )
        for slot in range(CAP)
    ]
    high, middle, low = three_parts(jnp.concatenate(slots, axis=0))
    return jnp.dot(collect, jnp.concatenate([high, middle, low], axis=0), preferred_element_type=F32)


def arrived_scalars(in_ref):
    peers = in_ref.shape[0] // DELIVER
    row = jnp.sum(in_ref[pl.ds(FETCH, peers, stride=DELIVER), :], axis=0, keepdims=True)
    return jnp.broadcast_to(row, (8, LANES))


def everywhere(values, lane):
    return jnp.broadcast_to(values[:, lane : lane + 1], (8, LANES))


def spanning(tile, shape):
    rows, columns = shape
    return jnp.concatenate([jnp.concatenate([tile] * (columns // LANES), axis=1)] * (rows // 8), axis=0)


def lane_sums(values):
    tiles = [
        values[row : row + 8, column : column + LANES]
        for row in range(0, values.shape[0], 8)
        for column in range(0, values.shape[1], LANES)
    ]
    while len(tiles) > 1:
        tiles = [sum(tiles[at : at + 2]) for at in range(0, len(tiles), 2)]
    return jnp.broadcast_to(jnp.sum(tiles[0], axis=1, keepdims=True), (8, LANES))


def in_lanes(sums, first=0):
    lanes = lane_ids((8, LANES))
    packed = jnp.zeros((8, LANES), F32)
    for lane, value in enumerate(sums, first):
        packed = jnp.where(lanes == lane, value, packed)
    return packed


def first_gather_kernel(in_ref, prior_ref, half_ref, collect_ref, pick_ref):
    peers = in_ref.shape[0] // DELIVER
    own, width = prior_ref.shape
    cells = CORES * own
    ids = in_ref[pl.ds(FETCH, peers, stride=DELIVER), :]
    lanes = lane_ids((peers, LANES)).astype(F32)
    pick = jnp.concatenate(
        [(ids[:, slot : slot + 1] == lanes + 1.0).astype(F32) for slot in range(CAP)], axis=0
    )
    pick = jnp.where(lane_ids(pick.shape) < cells, pick, 0.0)
    collect = jnp.concatenate([pick.T[:cells, :]] * 3, axis=1).astype(BF16)
    collect_ref[...] = collect
    folds = [pick[:, :cells]] * 3 + [jnp.zeros((pick.shape[0], cells), F32)]
    pick_ref[...] = jnp.concatenate(folds, axis=1).astype(BF16)
    half_ref[0:cells, :] = gathered(in_ref, collect)
    half_ref[cells : cells + own, :] = prior_ref[...]


def gather_kernel(in_ref, collect_ref, half_ref):
    cells = collect_ref.shape[0]
    half_ref[0:cells, :] = gathered(in_ref, collect_ref[...])
    scalars = arrived_scalars(in_ref)
    half_ref[cells : cells + 8, :] = jnp.concatenate([scalars, jnp.zeros_like(scalars)], axis=1)


def partial_sums(prior, residual, direction=None):
    halved = 0.5 * residual
    weighted = prior * halved
    values = [halved * residual, weighted * residual]
    if direction is not None:
        values.append(weighted * direction)
    return in_lanes([lane_sums(value) for value in values])


def first_update_kernel(mine_ref, other_ref, pick_ref, prior_ref, residual_ref, sums_ref, out_ref):
    cells = residual_ref.shape[0]
    own = cells // CORES
    first = lax.axis_index("orb") % CORES == 0
    mine = mine_ref[cells : cells + own, :]
    other = other_ref[cells : cells + own, :]
    prior = jnp.concatenate([jnp.where(first, mine, other), jnp.where(first, other, mine)], axis=0)
    prior_ref[...] = prior
    residual = mine_ref[0:cells, :] + other_ref[0:cells, :]
    residual_ref[...] = residual
    sums_ref[...] = partial_sums(prior, residual)
    serve(residual, pick_ref[...], out_ref)


def update_kernel(first, last, *refs):
    mine_ref, other_ref, pick_ref, prior_ref, residual_ref, *refs = refs
    if not first:
        state_ref, direction_ref, image_ref, solution_ref, *refs = refs
    cells, width = residual_ref.shape
    sums = mine_ref[cells : cells + 8, :LANES] + other_ref[cells : cells + 8, :LANES]
    norm, prior_rr, prior_rd, forward_rr, forward_rd = [everywhere(sums, at) for at in range(5)]
    prior = prior_ref[...]
    residual = residual_ref[...]
    image = mine_ref[0:cells, :] + other_ref[0:cells, :] + prior * residual
    direction, prior_dd, forward_dd = residual, prior_rr, forward_rr
    if not first:
        beta = norm / state_ref[0:8, :]
        prior_dd = prior_rr + beta * (2.0 * prior_rd + beta * state_ref[8:16, :])
        forward_dd = forward_rr + beta * (2.0 * forward_rd + beta * state_ref[16:24, :])
        wide = spanning(beta, (cells, width))
        direction = residual + wide * direction_ref[...]
        image = image + wide * image_ref[...]
    alpha = spanning(norm / (prior_dd + forward_dd), (cells, width))
    new_residual = residual - alpha * image
    solution = alpha * direction if first else solution_ref[...] + alpha * direction
    if last:
        new_solution_ref, new_residual_ref = refs
        own = cells // CORES
        core_first = lax.axis_index("orb") % CORES == 0
        new_solution_ref[...] = jnp.where(core_first, solution[:own], solution[own:])
        new_residual_ref[...] = jnp.where(core_first, new_residual[:own], new_residual[own:])
        return
    new_residual_ref, sums_ref, out_ref, new_state_ref, new_direction_ref, new_image_ref, new_solution_ref = refs
    serve(new_residual, pick_ref[...], out_ref)
    sums_ref[...] = partial_sums(prior, new_residual, direction)
    new_residual_ref[...] = new_residual
    new_state_ref[0:8, :] = norm
    new_state_ref[8:16, :] = prior_dd
    new_state_ref[16:24, :] = forward_dd
    new_state_ref[24:32, :] = jnp.zeros_like(norm) if first else beta
    new_direction_ref[...] = direction
    new_image_ref[...] = image
    new_solution_ref[...] = solution


def forward_kernel(meta_ref, in_ref, scalars_ref, footprint_ref, out_ref, sums_ref):
    blocks = footprint_ref.shape[0]
    rows, soundings, _ = sums_ref.shape
    sums_ref[...] = jnp.zeros_like(sums_ref)

    def product(block):
        row = meta_ref[blocks + block]
        place = meta_ref[2 * blocks + block]
        left = jnp.broadcast_to(in_ref[pl.ds(place, 1), :], (2 * SUB, LANES))
        right = jnp.broadcast_to(in_ref[pl.ds(place + 1, 1), :], (2 * SUB, LANES))
        for start in range(0, soundings, 2 * SUB):
            part = footprint_ref[block, start : start + 2 * SUB, :]
            sums_ref[row, start : start + 2 * SUB, :] += part[:, :LANES] * left + part[:, LANES:] * right

    each(0, blocks, 4, product)
    lanes = lane_ids((8, LANES))
    per_half = LANES // rows
    halves = []
    for half in range(soundings // 8 // per_half):
        packed = [jnp.zeros((8, LANES), F32) for _ in range(4)]
        for at in range(per_half):
            group = half * per_half + at
            for row in range(rows):
                summed = jnp.sum(sums_ref[row, 8 * group : 8 * group + 8, :], axis=1, keepdims=True)
                packed[row % 4] = jnp.where(lanes == rows * at + row, summed, packed[row % 4])
        halves.append((packed[0] + packed[1]) + (packed[2] + packed[3]))
    halves.append(scalars_ref[...])
    out_ref[...] = jnp.concatenate(halves, axis=0)


def adjoint_kernel(iteration, last, *refs):
    meta_ref, own_ref, next_ref, previous_ref, opposite_ref, weights_ref, footprint_ref, *refs = refs
    if iteration > 0:
        state_ref, old_ref, *refs = refs
    if iteration > 1:
        older_ref, *refs = refs
    out_ref, *refs = refs
    blocks = footprint_ref.shape[0]
    peers = out_ref.shape[0] // DELIVER
    summed = (own_ref[...] + opposite_ref[...]) + (next_ref[...] + previous_ref[...])
    forward = jnp.concatenate([summed[0:8], summed[8:16]], axis=1)
    field = weights_ref[...] * forward
    *refs, field_ref = refs
    out_ref[...] = jnp.zeros_like(out_ref)
    spread(field, field_ref)
    def product(block):
        transposed_product(
            footprint_ref, field_ref, out_ref, block, meta_ref[blocks + block], meta_ref[block]
        )

    together = 8
    each(0, blocks - together, together, product)
    sums = [lane_sums(field * forward)]
    if iteration > 0:
        direction = old_ref[...]
        if iteration > 1:
            direction = direction + spanning(state_ref[24:32, :], direction.shape) * older_ref[...]
        sums.append(lane_sums(field * direction))
    if not last:
        refs[0][...] = forward
        if iteration > 0:
            refs[1][...] = direction
    scalars = jnp.sum(summed[16:24] + in_lanes(sums, 3), axis=0, keepdims=True)
    out_ref[pl.ds(FETCH, peers, stride=DELIVER), :] = jnp.broadcast_to(scalars, (peers, LANES))
    for block in range(blocks - together, blocks):
        product(block)


def call(kernel, out_shape, kinds, out_kinds=None, scratch=()):
    spaces = {"v": pltpu.VMEM, "s": pltpu.SMEM, "h": pl.ANY}
    out_kinds = out_kinds or "v" * len(out_shape)
    return pl.pallas_call(
        kernel,
        out_shape=out_shape,
        in_specs=[pl.BlockSpec(memory_space=spaces[kind]) for kind in kinds],
        out_specs=[pl.BlockSpec(memory_space=spaces[kind]) for kind in out_kinds],
        scratch_shapes=list(scratch),
        compiler_params=pltpu.CompilerParams(vmem_limit_bytes=16 * 1024 * 1024),
    )


def per_device(observed, weights, precision_prior, footprint, block_rows, block_cells):
    rows, soundings = observed.shape
    own, width = precision_prior.shape
    cells = CORES * own
    blocks = footprint.shape[0]
    orbits = lax.axis_size("orb")
    reps = lax.axis_size("rep")
    peers = orbits // CORES
    shape = jax.ShapeDtypeStruct
    fetched = shape((peers * FETCH, LANES), F32)
    delivered = shape((peers * DELIVER, LANES), F32)
    packed_shape = shape((8, soundings * rows // 8), F32)
    scalar_shape = shape((8, LANES), F32)
    state_shape = shape((32, LANES), F32)
    region = shape((cells, width), F32)
    field = pltpu.VMEM((rows, soundings, LANES), F32)
    same_core = [[CORES * peer + core for peer in range(peers)] for core in range(CORES)]
    swapped = [(device, device ^ 1) for device in range(orbits)]

    def exchange(array):
        flat = array.reshape(peers, 1, array.shape[0] // peers * LANES)
        flat = lax.all_to_all(
            flat, "orb", split_axis=0, concat_axis=0, axis_index_groups=same_core, tiled=True
        )
        return flat.reshape(array.shape)

    def swap(array):
        return lax.ppermute(array, "orb", swapped)

    in_hbm = [
        pltpu.with_memory_space_constraint(array, pltpu.HBM)
        for array in (block_rows, block_cells, observed, weights, precision_prior, footprint)
    ]
    outgoing, meta, packed_weights, own_prior, footprint = call(
        functools.partial(start_kernel, cells),
        [
            delivered,
            pltpu.SMEM((3 * blocks,), jnp.int32),
            packed_shape,
            pltpu.VMEM(precision_prior.shape, F32),
            pltpu.VMEM(footprint.shape, F32),
        ],
        "hhhhhh",
        "vsvvv",
        [
            pltpu.VMEM(footprint.shape, footprint.dtype),
            field,
            pltpu.SMEM((peers,), jnp.int32),
            pltpu.SMEM((blocks,), jnp.int32),
            pltpu.SMEM((blocks,), jnp.int32),
            pltpu.VMEM(observed.shape, F32),
            pltpu.VMEM(weights.shape, F32),
            pltpu.SemaphoreType.DMA((5,)),
            pltpu.SemaphoreType.DMA((12,)),
        ],
    )(*in_hbm)
    half, collect, pick = call(
        first_gather_kernel,
        [
            shape((cells + own, width), F32),
            shape((cells, 3 * CAP * peers), BF16),
            shape((CAP * peers, 4 * cells), BF16),
        ],
        "vv",
    )(exchange(outgoing), own_prior)
    prior, residual, sums, outgoing = call(
        first_update_kernel, [region, region, scalar_shape, fetched], "vvv"
    )(half, swap(half), pick)
    state, history, images = None, (), ()
    for iteration in range(ITERS):
        first, last = iteration == 0, iteration == ITERS - 1
        (partial,) = call(
            forward_kernel, [shape((24, LANES), F32)], "svvv", scratch=[field]
        )(meta, exchange(outgoing), sums, footprint)
        others = [
            lax.ppermute(partial, "rep", [(device, device ^ by) for device in range(reps)])
            for by in (1, 3, 2)
        ]
        operands = [meta, partial, *others, packed_weights, footprint]
        operands += [] if first else [state, *images]
        outgoing, *images = call(
            functools.partial(adjoint_kernel, iteration, last),
            [delivered] + ([] if last else [packed_shape] * (1 if first else 2)),
            "s" + "v" * (len(operands) - 1),
            scratch=[field],
        )(*operands)
        (half,) = call(gather_kernel, [shape((cells + 8, width), F32)], "vv")(
            exchange(outgoing), collect
        )
        operands = [half, swap(half), pick, prior, residual]
        operands += [] if first else [state, *history]
        results = call(
            functools.partial(update_kernel, first, last),
            [shape((own, width), F32)] * 2
            if last
            else [region, scalar_shape, fetched, state_shape, region, region, region],
            "v" * len(operands),
        )(*operands)
        if not last:
            residual, sums, outgoing, state, *history = results
    return tuple(results)


def solution(mesh):
    in_specs = (
        P("orb", None),
        P("orb", None),
        P("orb", "rep"),
        P("orb", None, "rep"),
        P("orb"),
        P("orb"),
    )
    out_specs = (P("orb", "rep"), P("orb", "rep"))
    return jax.shard_map(
        per_device, mesh=mesh, in_specs=in_specs, out_specs=out_specs, check_vma=False
    )
```

```python
import functools

import jax
import jax.numpy as jnp
from jax import lax
from jax.experimental import pallas as pl
from jax.experimental.pallas import tpu as pltpu
from jax.sharding import PartitionSpec as P

ITERS = 4
CORES = 2
CAP = 2 * CORES
FETCH = 2 * CAP
DELIVER = FETCH + 1
LANES = 128
SUB = 16
IN_FLIGHT = 6
F32 = jnp.float32
BF16 = jnp.bfloat16


def lane_ids(shape):
    return lax.broadcasted_iota(jnp.int32, shape, len(shape) - 1)


def three_parts(values):
    high = values.astype(BF16)
    rest = values - high.astype(F32)
    middle = rest.astype(BF16)
    low = (rest - middle.astype(F32)).astype(BF16)
    return high, middle, low


def spread(packed, field_ref):
    rows, soundings, _ = field_ref.shape
    columns = []
    for group in range(soundings // 8):
        start = rows * group // LANES * LANES
        shift = rows * group % LANES
        half = packed[:, start : start + LANES]
        columns.append(pltpu.roll(half, LANES - shift, 1) if shift else half)
    high, middle, _ = three_parts(jnp.concatenate(columns, axis=0))
    parts = jnp.concatenate([high, middle], axis=1)
    source = lax.broadcasted_iota(jnp.int32, (2 * LANES, 2 * LANES), 0) % LANES
    target = lane_ids((2 * LANES, 2 * LANES)) // LANES
    for row in range(0, rows, 2):
        pick = jnp.where(source == row + target, 1.0, 0.0).astype(BF16)
        pair = jnp.dot(parts, pick, preferred_element_type=F32)
        field_ref[row] = pair[:, :LANES]
        field_ref[row + 1] = pair[:, LANES:]


def transposed_product(footprint_ref, field_ref, out_ref, block, row, place, keep_ref=None):
    soundings = footprint_ref.shape[1]
    left = jnp.zeros((SUB, LANES), F32)
    right = jnp.zeros((SUB, LANES), F32)
    for start in range(0, soundings, SUB):
        part = footprint_ref[block, start : start + SUB, :].astype(F32)
        if keep_ref is not None:
            keep_ref[block, start : start + SUB, :] = part
        z = field_ref[row, start : start + SUB, :]
        left = left + part[:, :LANES] * z
        right = right + part[:, LANES:] * z
    out_ref[pl.ds(place, 1), :] = jnp.sum(left, axis=0, keepdims=True)
    out_ref[pl.ds(place + 1, 1), :] = jnp.sum(right, axis=0, keepdims=True)


def each(first, last, together, do):
    def body(step, carry):
        for at in range(together):
            do(first + step * together + at)
        return carry

    lax.fori_loop(0, (last - first) // together, body, 0)


def in_columns(values):
    rows, soundings = values.shape
    parts = []
    for start in range(0, soundings, LANES):
        part = values[:, start : start + LANES]
        parts.append(jnp.concatenate([part] * (LANES // rows), axis=0).T)
    return jnp.concatenate(parts, axis=0)


def start_kernel(
    cells, rows_hbm, cells_hbm, observed_hbm, weights_hbm, prior_hbm, footprint_hbm,
    out_ref, meta_ref, packed_ref, prior_ref, footprint_ref,
    arrived_ref, field_ref, count_ref, rows_ref, cells_ref, observed_ref, weights_ref, sems, chunk_sems
):
    blocks = footprint_ref.shape[0]
    rows, soundings = weights_ref.shape
    peers = out_ref.shape[0] // DELIVER
    chunks = chunk_sems.shape[0]
    shift = cells.bit_length() - 1
    assert cells == 1 << shift and rows & (rows - 1) == 0
    size = blocks // chunks
    small = [
        pltpu.make_async_copy(source, target, sems.at[at])
        for at, (source, target) in enumerate(
            [
                (rows_hbm, rows_ref),
                (cells_hbm, cells_ref),
                (observed_hbm, observed_ref),
                (weights_hbm, weights_ref),
                (prior_hbm, prior_ref),
            ]
        )
    ]
    for copy in small:
        copy.start()
    large = []
    for chunk in range(chunks):
        span = pl.ds(chunk * size, size)
        large.append(
            pltpu.make_async_copy(footprint_hbm.at[span], arrived_ref.at[span], chunk_sems.at[chunk])
        )
    for copy in large[:IN_FLIGHT]:
        copy.start()
    out_ref[...] = jnp.zeros_like(out_ref)
    for peer in range(peers):
        count_ref[peer] = 0
    for copy in small[:-1]:
        copy.wait()
    weights = weights_ref[...]
    columns = in_columns(weights * observed_ref[...])
    for row in range(rows):
        field_ref[row] = jnp.broadcast_to(columns[:, row : row + 1], (soundings, LANES))
    columns = in_columns(weights)
    groups = LANES // rows
    lanes = lane_ids((8, LANES)) // rows
    for half in range(soundings // LANES):
        packed = jnp.zeros((8, LANES), F32)
        for at in range(groups):
            start = half * LANES + 8 * at
            packed = jnp.where(lanes == at, columns[start : start + 8, :], packed)
        packed_ref[:, half * LANES : (half + 1) * LANES] = packed

    def product(block):
        cell = cells_ref[block]
        peer = lax.shift_right_logical(cell, shift)
        slot = cell & (cells - 1)
        rank = count_ref[peer]
        count_ref[peer] = rank + 1
        row = rows_ref[block] & (rows - 1)
        place = peer * DELIVER + 2 * rank
        meta_ref[block] = place
        meta_ref[blocks + block] = row
        meta_ref[2 * blocks + block] = peer * FETCH + 2 * rank
        pltpu.store(
            out_ref.at[pl.ds(peer * DELIVER + FETCH, 1), :],
            jnp.full((1, LANES), (slot + 1).astype(F32)),
            mask=lane_ids((1, LANES)) == rank,
        )
        transposed_product(arrived_ref, field_ref, out_ref, block, row, place, footprint_ref)

    for chunk in range(chunks):
        large[chunk].wait()
        if chunk + IN_FLIGHT < chunks:
            large[chunk + IN_FLIGHT].start()
        each(chunk * size, (chunk + 1) * size, 4, product)
    small[-1].wait()


def serve(residual, pick, out_ref):
    peers = out_ref.shape[0] // FETCH
    high, middle, low = three_parts(residual)
    stacked = jnp.concatenate([high, middle, low, jnp.zeros_like(high)], axis=0)
    pieces = jnp.dot(pick, stacked, preferred_element_type=F32)
    for slot in range(CAP):
        for half in range(2):
            out_ref[pl.ds(2 * slot + half, peers, stride=FETCH), :] = pieces[
                slot * peers : (slot + 1) * peers, half * LANES : (half + 1) * LANES
            ]


def gathered(in_ref, collect):
    peers = in_ref.shape[0] // DELIVER
    slots = [
        jnp.concatenate(
            [in_ref[pl.ds(2 * slot + half, peers, stride=DELIVER), :] for half in range(2)], axis=1
        )
        for slot in range(CAP)
    ]
    high, middle, low = three_parts(jnp.concatenate(slots, axis=0))
    return jnp.dot(collect, jnp.concatenate([high, middle, low], axis=0), preferred_element_type=F32)


def arrived_scalars(in_ref):
    peers = in_ref.shape[0] // DELIVER
    row = jnp.sum(in_ref[pl.ds(FETCH, peers, stride=DELIVER), :], axis=0, keepdims=True)
    return jnp.broadcast_to(row, (8, LANES))


def everywhere(values, lane):
    return jnp.broadcast_to(values[:, lane : lane + 1], (8, LANES))


def spanning(tile, shape):
    rows, columns = shape
    return jnp.concatenate([jnp.concatenate([tile] * (columns // LANES), axis=1)] * (rows // 8), axis=0)


def lane_sums(values):
    tiles = [
        values[row : row + 8, column : column + LANES]
        for row in range(0, values.shape[0], 8)
        for column in range(0, values.shape[1], LANES)
    ]
    while len(tiles) > 1:
        tiles = [sum(tiles[at : at + 2]) for at in range(0, len(tiles), 2)]
    return jnp.broadcast_to(jnp.sum(tiles[0], axis=1, keepdims=True), (8, LANES))


def in_lanes(sums, first=0):
    lanes = lane_ids((8, LANES))
    packed = jnp.zeros((8, LANES), F32)
    for lane, value in enumerate(sums, first):
        packed = jnp.where(lanes == lane, value, packed)
    return packed


def first_gather_kernel(in_ref, prior_ref, half_ref, collect_ref, pick_ref):
    peers = in_ref.shape[0] // DELIVER
    own, width = prior_ref.shape
    cells = CORES * own
    ids = in_ref[pl.ds(FETCH, peers, stride=DELIVER), :]
    lanes = lane_ids((peers, LANES)).astype(F32)
    pick = jnp.concatenate(
        [(ids[:, slot : slot + 1] == lanes + 1.0).astype(F32) for slot in range(CAP)], axis=0
    )
    pick = jnp.where(lane_ids(pick.shape) < cells, pick, 0.0)
    collect = jnp.concatenate([pick.T[:cells, :]] * 3, axis=1).astype(BF16)
    collect_ref[...] = collect
    folds = [pick[:, :cells]] * 3 + [jnp.zeros((pick.shape[0], cells), F32)]
    pick_ref[...] = jnp.concatenate(folds, axis=1).astype(BF16)
    half_ref[0:cells, :] = gathered(in_ref, collect)
    half_ref[cells : cells + own, :] = prior_ref[...]


def gather_kernel(in_ref, collect_ref, half_ref):
    cells = collect_ref.shape[0]
    half_ref[0:cells, :] = gathered(in_ref, collect_ref[...])
    scalars = arrived_scalars(in_ref)
    half_ref[cells : cells + 8, :] = jnp.concatenate([scalars, jnp.zeros_like(scalars)], axis=1)


def partial_sums(prior, residual, direction=None):
    halved = 0.5 * residual
    weighted = prior * halved
    values = [halved * residual, weighted * residual]
    if direction is not None:
        values.append(weighted * direction)
    return in_lanes([lane_sums(value) for value in values])


def first_update_kernel(mine_ref, other_ref, pick_ref, prior_ref, residual_ref, sums_ref, out_ref):
    cells = residual_ref.shape[0]
    own = cells // CORES
    first = lax.axis_index("orb") % CORES == 0
    mine = mine_ref[cells : cells + own, :]
    other = other_ref[cells : cells + own, :]
    prior = jnp.concatenate([jnp.where(first, mine, other), jnp.where(first, other, mine)], axis=0)
    prior_ref[...] = prior
    residual = mine_ref[0:cells, :] + other_ref[0:cells, :]
    residual_ref[...] = residual
    sums_ref[...] = partial_sums(prior, residual)
    serve(residual, pick_ref[...], out_ref)


def update_kernel(first, last, *refs):
    mine_ref, other_ref, pick_ref, prior_ref, residual_ref, *refs = refs
    if not first:
        state_ref, direction_ref, image_ref, solution_ref, *refs = refs
    cells, width = residual_ref.shape
    sums = mine_ref[cells : cells + 8, :LANES] + other_ref[cells : cells + 8, :LANES]
    norm, prior_rr, prior_rd, forward_rr, forward_rd = [everywhere(sums, at) for at in range(5)]
    prior = prior_ref[...]
    residual = residual_ref[...]
    image = mine_ref[0:cells, :] + other_ref[0:cells, :] + prior * residual
    direction, prior_dd, forward_dd = residual, prior_rr, forward_rr
    if not first:
        beta = norm / state_ref[0:8, :]
        prior_dd = prior_rr + beta * (2.0 * prior_rd + beta * state_ref[8:16, :])
        forward_dd = forward_rr + beta * (2.0 * forward_rd + beta * state_ref[16:24, :])
        wide = spanning(beta, (cells, width))
        direction = residual + wide * direction_ref[...]
        image = image + wide * image_ref[...]
    alpha = spanning(norm / (prior_dd + forward_dd), (cells, width))
    new_residual = residual - alpha * image
    solution = alpha * direction if first else solution_ref[...] + alpha * direction
    if last:
        new_solution_ref, new_residual_ref = refs
        own = cells // CORES
        core_first = lax.axis_index("orb") % CORES == 0
        new_solution_ref[...] = jnp.where(core_first, solution[:own], solution[own:])
        new_residual_ref[...] = jnp.where(core_first, new_residual[:own], new_residual[own:])
        return
    new_residual_ref, sums_ref, out_ref, new_state_ref, new_direction_ref, new_image_ref, new_solution_ref = refs
    serve(new_residual, pick_ref[...], out_ref)
    sums_ref[...] = partial_sums(prior, new_residual, direction)
    new_residual_ref[...] = new_residual
    new_state_ref[0:8, :] = norm
    new_state_ref[8:16, :] = prior_dd
    new_state_ref[16:24, :] = forward_dd
    new_state_ref[24:32, :] = jnp.zeros_like(norm) if first else beta
    new_direction_ref[...] = direction
    new_image_ref[...] = image
    new_solution_ref[...] = solution


def forward_kernel(meta_ref, in_ref, scalars_ref, footprint_ref, out_ref, sums_ref):
    blocks = footprint_ref.shape[0]
    rows, soundings, _ = sums_ref.shape
    sums_ref[...] = jnp.zeros_like(sums_ref)

    def product(block):
        row = meta_ref[blocks + block]
        place = meta_ref[2 * blocks + block]
        left = jnp.broadcast_to(in_ref[pl.ds(place, 1), :], (2 * SUB, LANES))
        right = jnp.broadcast_to(in_ref[pl.ds(place + 1, 1), :], (2 * SUB, LANES))
        for start in range(0, soundings, 2 * SUB):
            part = footprint_ref[block, start : start + 2 * SUB, :]
            sums_ref[row, start : start + 2 * SUB, :] += part[:, :LANES] * left + part[:, LANES:] * right

    each(0, blocks, 8, product)
    lanes = lane_ids((8, LANES))
    per_half = LANES // rows
    halves = []
    for half in range(soundings // 8 // per_half):
        packed = [jnp.zeros((8, LANES), F32) for _ in range(4)]
        for at in range(per_half):
            group = half * per_half + at
            for row in range(rows):
                summed = jnp.sum(sums_ref[row, 8 * group : 8 * group + 8, :], axis=1, keepdims=True)
                packed[row % 4] = jnp.where(lanes == rows * at + row, summed, packed[row % 4])
        halves.append((packed[0] + packed[1]) + (packed[2] + packed[3]))
    halves.append(scalars_ref[...])
    out_ref[...] = jnp.concatenate(halves, axis=0)


def adjoint_kernel(iteration, last, *refs):
    meta_ref, own_ref, next_ref, previous_ref, opposite_ref, weights_ref, footprint_ref, *refs = refs
    if iteration > 0:
        state_ref, old_ref, *refs = refs
    if iteration > 1:
        older_ref, *refs = refs
    out_ref, *refs = refs
    blocks = footprint_ref.shape[0]
    peers = out_ref.shape[0] // DELIVER
    summed = (own_ref[...] + opposite_ref[...]) + (next_ref[...] + previous_ref[...])
    forward = jnp.concatenate([summed[0:8], summed[8:16]], axis=1)
    field = weights_ref[...] * forward
    *refs, field_ref = refs
    out_ref[...] = jnp.zeros_like(out_ref)
    spread(field, field_ref)
    def product(block):
        transposed_product(
            footprint_ref, field_ref, out_ref, block, meta_ref[blocks + block], meta_ref[block]
        )

    together = 8
    each(0, blocks - together, together, product)
    sums = [lane_sums(field * forward)]
    if iteration > 0:
        direction = old_ref[...]
        if iteration > 1:
            direction = direction + spanning(state_ref[24:32, :], direction.shape) * older_ref[...]
        sums.append(lane_sums(field * direction))
    if not last:
        refs[0][...] = forward
        if iteration > 0:
            refs[1][...] = direction
    scalars = jnp.sum(summed[16:24] + in_lanes(sums, 3), axis=0, keepdims=True)
    out_ref[pl.ds(FETCH, peers, stride=DELIVER), :] = jnp.broadcast_to(scalars, (peers, LANES))
    for block in range(blocks - together, blocks):
        product(block)


def call(kernel, out_shape, kinds, out_kinds=None, scratch=()):
    spaces = {"v": pltpu.VMEM, "s": pltpu.SMEM, "h": pl.ANY}
    out_kinds = out_kinds or "v" * len(out_shape)
    return pl.pallas_call(
        kernel,
        out_shape=out_shape,
        in_specs=[pl.BlockSpec(memory_space=spaces[kind]) for kind in kinds],
        out_specs=[pl.BlockSpec(memory_space=spaces[kind]) for kind in out_kinds],
        scratch_shapes=list(scratch),
        compiler_params=pltpu.CompilerParams(vmem_limit_bytes=16 * 1024 * 1024),
    )


def per_device(observed, weights, precision_prior, footprint, block_rows, block_cells):
    rows, soundings = observed.shape
    own, width = precision_prior.shape
    cells = CORES * own
    blocks = footprint.shape[0]
    orbits = lax.axis_size("orb")
    reps = lax.axis_size("rep")
    peers = orbits // CORES
    shape = jax.ShapeDtypeStruct
    fetched = shape((peers * FETCH, LANES), F32)
    delivered = shape((peers * DELIVER, LANES), F32)
    packed_shape = shape((8, soundings * rows // 8), F32)
    scalar_shape = shape((8, LANES), F32)
    state_shape = shape((32, LANES), F32)
    region = shape((cells, width), F32)
    field = pltpu.VMEM((rows, soundings, LANES), F32)
    same_core = [[CORES * peer + core for peer in range(peers)] for core in range(CORES)]
    swapped = [(device, device ^ 1) for device in range(orbits)]

    def exchange(array):
        flat = array.reshape(peers, 1, array.shape[0] // peers * LANES)
        flat = lax.all_to_all(
            flat, "orb", split_axis=0, concat_axis=0, axis_index_groups=same_core, tiled=True
        )
        return flat.reshape(array.shape)

    def swap(array):
        return lax.ppermute(array, "orb", swapped)

    in_hbm = [
        pltpu.with_memory_space_constraint(array, pltpu.HBM)
        for array in (block_rows, block_cells, observed, weights, precision_prior, footprint)
    ]
    outgoing, meta, packed_weights, own_prior, footprint = call(
        functools.partial(start_kernel, cells),
        [
            delivered,
            pltpu.SMEM((3 * blocks,), jnp.int32),
            packed_shape,
            pltpu.VMEM(precision_prior.shape, F32),
            pltpu.VMEM(footprint.shape, F32),
        ],
        "hhhhhh",
        "vsvvv",
        [
            pltpu.VMEM(footprint.shape, footprint.dtype),
            field,
            pltpu.SMEM((peers,), jnp.int32),
            pltpu.SMEM((blocks,), jnp.int32),
            pltpu.SMEM((blocks,), jnp.int32),
            pltpu.VMEM(observed.shape, F32),
            pltpu.VMEM(weights.shape, F32),
            pltpu.SemaphoreType.DMA((5,)),
            pltpu.SemaphoreType.DMA((12,)),
        ],
    )(*in_hbm)
    half, collect, pick = call(
        first_gather_kernel,
        [
            shape((cells + own, width), F32),
            shape((cells, 3 * CAP * peers), BF16),
            shape((CAP * peers, 4 * cells), BF16),
        ],
        "vv",
    )(exchange(outgoing), own_prior)
    prior, residual, sums, outgoing = call(
        first_update_kernel, [region, region, scalar_shape, fetched], "vvv"
    )(half, swap(half), pick)
    state, history, images = None, (), ()
    for iteration in range(ITERS):
        first, last = iteration == 0, iteration == ITERS - 1
        (partial,) = call(
            forward_kernel, [shape((24, LANES), F32)], "svvv", scratch=[field]
        )(meta, exchange(outgoing), sums, footprint)
        others = [
            lax.ppermute(partial, "rep", [(device, device ^ by) for device in range(reps)])
            for by in (1, 3, 2)
        ]
        operands = [meta, partial, *others, packed_weights, footprint]
        operands += [] if first else [state, *images]
        outgoing, *images = call(
            functools.partial(adjoint_kernel, iteration, last),
            [delivered] + ([] if last else [packed_shape] * (1 if first else 2)),
            "s" + "v" * (len(operands) - 1),
            scratch=[field],
        )(*operands)
        (half,) = call(gather_kernel, [shape((cells + 8, width), F32)], "vv")(
            exchange(outgoing), collect
        )
        operands = [half, swap(half), pick, prior, residual]
        operands += [] if first else [state, *history]
        results = call(
            functools.partial(update_kernel, first, last),
            [shape((own, width), F32)] * 2
            if last
            else [region, scalar_shape, fetched, state_shape, region, region, region],
            "v" * len(operands),
        )(*operands)
        if not last:
            residual, sums, outgoing, state, *history = results
    return tuple(results)


def solution(mesh):
    in_specs = (
        P("orb", None),
        P("orb", None),
        P("orb", "rep"),
        P("orb", None, "rep"),
        P("orb"),
        P("orb"),
    )
    out_specs = (P("orb", "rep"), P("orb", "rep"))
    return jax.shard_map(
        per_device, mesh=mesh, in_specs=in_specs, out_specs=out_specs, check_vma=False
    )
```

```python
import functools

import jax
import jax.numpy as jnp
from jax import lax
from jax.experimental import pallas as pl
from jax.experimental.pallas import tpu as pltpu
from jax.sharding import PartitionSpec as P

ITERS = 4
CORES = 2
CAP = 2 * CORES
FETCH = 2 * CAP
DELIVER = FETCH + 1
LANES = 128
SUB = 16
IN_FLIGHT = 6
F32 = jnp.float32
BF16 = jnp.bfloat16


def lane_ids(shape):
    return lax.broadcasted_iota(jnp.int32, shape, len(shape) - 1)


def three_parts(values):
    high = values.astype(BF16)
    rest = values - high.astype(F32)
    middle = rest.astype(BF16)
    low = (rest - middle.astype(F32)).astype(BF16)
    return high, middle, low


def spread(packed, field_ref):
    rows, soundings, _ = field_ref.shape
    columns = []
    for group in range(soundings // 8):
        start = rows * group // LANES * LANES
        shift = rows * group % LANES
        half = packed[:, start : start + LANES]
        columns.append(pltpu.roll(half, LANES - shift, 1) if shift else half)
    spread_columns(jnp.concatenate(columns, axis=0), field_ref)


def spread_columns(columns, field_ref):
    rows = field_ref.shape[0]
    high, middle, _ = three_parts(columns)
    parts = jnp.concatenate([high, middle], axis=1)
    source = lax.broadcasted_iota(jnp.int32, (2 * LANES, 2 * LANES), 0) % LANES
    target = lane_ids((2 * LANES, 2 * LANES)) // LANES
    for row in range(0, rows, 2):
        pick = jnp.where(source == row + target, 1.0, 0.0).astype(BF16)
        pair = jnp.dot(parts, pick, preferred_element_type=F32)
        field_ref[row] = pair[:, :LANES]
        field_ref[row + 1] = pair[:, LANES:]


def transposed_product(footprint_ref, field_ref, out_ref, block, row, place, keep_ref=None):
    soundings = footprint_ref.shape[1]
    left = jnp.zeros((SUB, LANES), F32)
    right = jnp.zeros((SUB, LANES), F32)
    for start in range(0, soundings, SUB):
        part = footprint_ref[block, start : start + SUB, :].astype(F32)
        if keep_ref is not None:
            keep_ref[block, start : start + SUB, :] = part
        z = field_ref[row, start : start + SUB, :]
        left = left + part[:, :LANES] * z
        right = right + part[:, LANES:] * z
    out_ref[pl.ds(place, 1), :] = jnp.sum(left, axis=0, keepdims=True)
    out_ref[pl.ds(place + 1, 1), :] = jnp.sum(right, axis=0, keepdims=True)


def each(first, last, together, do):
    def body(step, carry):
        for at in range(together):
            do(first + step * together + at)
        return carry

    lax.fori_loop(0, (last - first) // together, body, 0)


def in_columns(values):
    rows, soundings = values.shape
    parts = []
    for start in range(0, soundings, LANES):
        part = values[:, start : start + LANES]
        parts.append(jnp.concatenate([part] * (LANES // rows), axis=0).T)
    return jnp.concatenate(parts, axis=0)


def start_kernel(
    cells, rows_hbm, cells_hbm, observed_hbm, weights_hbm, prior_hbm, footprint_hbm,
    out_ref, meta_ref, packed_ref, prior_ref, footprint_ref,
    arrived_ref, field_ref, count_ref, rows_ref, cells_ref, observed_ref, weights_ref, sems, chunk_sems
):
    blocks = footprint_ref.shape[0]
    rows, soundings = weights_ref.shape
    peers = out_ref.shape[0] // DELIVER
    chunks = chunk_sems.shape[0]
    shift = cells.bit_length() - 1
    assert cells == 1 << shift and rows & (rows - 1) == 0
    size = blocks // chunks
    small = [
        pltpu.make_async_copy(source, target, sems.at[at])
        for at, (source, target) in enumerate(
            [
                (rows_hbm, rows_ref),
                (cells_hbm, cells_ref),
                (observed_hbm, observed_ref),
                (weights_hbm, weights_ref),
                (prior_hbm, prior_ref),
            ]
        )
    ]
    for copy in small:
        copy.start()
    large = []
    for chunk in range(chunks):
        span = pl.ds(chunk * size, size)
        large.append(
            pltpu.make_async_copy(footprint_hbm.at[span], arrived_ref.at[span], chunk_sems.at[chunk])
        )
    for copy in large[:IN_FLIGHT]:
        copy.start()
    out_ref[...] = jnp.zeros_like(out_ref)
    for peer in range(peers):
        count_ref[peer] = 0
    for copy in small[:-1]:
        copy.wait()
    weights = weights_ref[...]
    spread_columns(in_columns(weights * observed_ref[...]), field_ref)
    columns = in_columns(weights)
    groups = LANES // rows
    lanes = lane_ids((8, LANES)) // rows
    for half in range(soundings // LANES):
        packed = jnp.zeros((8, LANES), F32)
        for at in range(groups):
            start = half * LANES + 8 * at
            packed = jnp.where(lanes == at, columns[start : start + 8, :], packed)
        packed_ref[:, half * LANES : (half + 1) * LANES] = packed

    def product(block):
        cell = cells_ref[block]
        peer = lax.shift_right_logical(cell, shift)
        slot = cell & (cells - 1)
        rank = count_ref[peer]
        count_ref[peer] = rank + 1
        row = rows_ref[block] & (rows - 1)
        place = peer * DELIVER + 2 * rank
        meta_ref[block] = place
        meta_ref[blocks + block] = row
        meta_ref[2 * blocks + block] = peer * FETCH + 2 * rank
        pltpu.store(
            out_ref.at[pl.ds(peer * DELIVER + FETCH, 1), :],
            jnp.full((1, LANES), (slot + 1).astype(F32)),
            mask=lane_ids((1, LANES)) == rank,
        )
        transposed_product(arrived_ref, field_ref, out_ref, block, row, place, footprint_ref)

    for chunk in range(chunks):
        large[chunk].wait()
        if chunk + IN_FLIGHT < chunks:
            large[chunk + IN_FLIGHT].start()
        each(chunk * size, (chunk + 1) * size, 4, product)
    small[-1].wait()


def serve(residual, pick, out_ref):
    peers = out_ref.shape[0] // FETCH
    high, middle, low = three_parts(residual)
    stacked = jnp.concatenate([high, middle, low, jnp.zeros_like(high)], axis=0)
    pieces = jnp.dot(pick, stacked, preferred_element_type=F32)
    for slot in range(CAP):
        for half in range(2):
            out_ref[pl.ds(2 * slot + half, peers, stride=FETCH), :] = pieces[
                slot * peers : (slot + 1) * peers, half * LANES : (half + 1) * LANES
            ]


def gathered(in_ref, collect):
    peers = in_ref.shape[0] // DELIVER
    slots = [
        jnp.concatenate(
            [in_ref[pl.ds(2 * slot + half, peers, stride=DELIVER), :] for half in range(2)], axis=1
        )
        for slot in range(CAP)
    ]
    high, middle, low = three_parts(jnp.concatenate(slots, axis=0))
    return jnp.dot(collect, jnp.concatenate([high, middle, low], axis=0), preferred_element_type=F32)


def arrived_scalars(in_ref):
    peers = in_ref.shape[0] // DELIVER
    row = jnp.sum(in_ref[pl.ds(FETCH, peers, stride=DELIVER), :], axis=0, keepdims=True)
    return jnp.broadcast_to(row, (8, LANES))


def everywhere(values, lane):
    return jnp.broadcast_to(values[:, lane : lane + 1], (8, LANES))


def spanning(tile, shape):
    rows, columns = shape
    return jnp.concatenate([jnp.concatenate([tile] * (columns // LANES), axis=1)] * (rows // 8), axis=0)


def lane_sums(values):
    tiles = [
        values[row : row + 8, column : column + LANES]
        for row in range(0, values.shape[0], 8)
        for column in range(0, values.shape[1], LANES)
    ]
    while len(tiles) > 1:
        tiles = [sum(tiles[at : at + 2]) for at in range(0, len(tiles), 2)]
    return jnp.broadcast_to(jnp.sum(tiles[0], axis=1, keepdims=True), (8, LANES))


def in_lanes(sums, first=0):
    lanes = lane_ids((8, LANES))
    packed = jnp.zeros((8, LANES), F32)
    for lane, value in enumerate(sums, first):
        packed = jnp.where(lanes == lane, value, packed)
    return packed


def first_gather_kernel(in_ref, prior_ref, half_ref, collect_ref, pick_ref):
    peers = in_ref.shape[0] // DELIVER
    own, width = prior_ref.shape
    cells = CORES * own
    ids = in_ref[pl.ds(FETCH, peers, stride=DELIVER), :]
    lanes = lane_ids((peers, LANES)).astype(F32)
    pick = jnp.concatenate(
        [(ids[:, slot : slot + 1] == lanes + 1.0).astype(F32) for slot in range(CAP)], axis=0
    )
    pick = jnp.where(lane_ids(pick.shape) < cells, pick, 0.0)
    collect = jnp.concatenate([pick.T[:cells, :]] * 3, axis=1).astype(BF16)
    collect_ref[...] = collect
    folds = [pick[:, :cells]] * 3 + [jnp.zeros((pick.shape[0], cells), F32)]
    pick_ref[...] = jnp.concatenate(folds, axis=1).astype(BF16)
    half_ref[0:cells, :] = gathered(in_ref, collect)
    half_ref[cells : cells + own, :] = prior_ref[...]


def gather_kernel(in_ref, collect_ref, half_ref):
    cells = collect_ref.shape[0]
    half_ref[0:cells, :] = gathered(in_ref, collect_ref[...])
    scalars = arrived_scalars(in_ref)
    half_ref[cells : cells + 8, :] = jnp.concatenate([scalars, jnp.zeros_like(scalars)], axis=1)


def partial_sums(prior, residual, direction=None):
    halved = 0.5 * residual
    weighted = prior * halved
    values = [halved * residual, weighted * residual]
    if direction is not None:
        values.append(weighted * direction)
    return in_lanes([lane_sums(value) for value in values])


def first_update_kernel(mine_ref, other_ref, pick_ref, prior_ref, residual_ref, sums_ref, out_ref):
    cells = residual_ref.shape[0]
    own = cells // CORES
    first = lax.axis_index("orb") % CORES == 0
    mine = mine_ref[cells : cells + own, :]
    other = other_ref[cells : cells + own, :]
    prior = jnp.concatenate([jnp.where(first, mine, other), jnp.where(first, other, mine)], axis=0)
    prior_ref[...] = prior
    residual = mine_ref[0:cells, :] + other_ref[0:cells, :]
    residual_ref[...] = residual
    sums_ref[...] = partial_sums(prior, residual)
    serve(residual, pick_ref[...], out_ref)


def update_kernel(first, last, *refs):
    mine_ref, other_ref, pick_ref, prior_ref, residual_ref, *refs = refs
    if not first:
        state_ref, direction_ref, image_ref, solution_ref, *refs = refs
    cells, width = residual_ref.shape
    sums = mine_ref[cells : cells + 8, :LANES] + other_ref[cells : cells + 8, :LANES]
    norm, prior_rr, prior_rd, forward_rr, forward_rd = [everywhere(sums, at) for at in range(5)]
    prior = prior_ref[...]
    residual = residual_ref[...]
    image = mine_ref[0:cells, :] + other_ref[0:cells, :] + prior * residual
    direction, prior_dd, forward_dd = residual, prior_rr, forward_rr
    if not first:
        beta = norm / state_ref[0:8, :]
        prior_dd = prior_rr + beta * (2.0 * prior_rd + beta * state_ref[8:16, :])
        forward_dd = forward_rr + beta * (2.0 * forward_rd + beta * state_ref[16:24, :])
        wide = spanning(beta, (cells, width))
        direction = residual + wide * direction_ref[...]
        image = image + wide * image_ref[...]
    alpha = spanning(norm / (prior_dd + forward_dd), (cells, width))
    new_residual = residual - alpha * image
    solution = alpha * direction if first else solution_ref[...] + alpha * direction
    if last:
        new_solution_ref, new_residual_ref = refs
        own = cells // CORES
        core_first = lax.axis_index("orb") % CORES == 0
        new_solution_ref[...] = jnp.where(core_first, solution[:own], solution[own:])
        new_residual_ref[...] = jnp.where(core_first, new_residual[:own], new_residual[own:])
        return
    new_residual_ref, sums_ref, out_ref, new_state_ref, new_direction_ref, new_image_ref, new_solution_ref = refs
    serve(new_residual, pick_ref[...], out_ref)
    sums_ref[...] = partial_sums(prior, new_residual, direction)
    new_residual_ref[...] = new_residual
    new_state_ref[0:8, :] = norm
    new_state_ref[8:16, :] = prior_dd
    new_state_ref[16:24, :] = forward_dd
    new_state_ref[24:32, :] = jnp.zeros_like(norm) if first else beta
    new_direction_ref[...] = direction
    new_image_ref[...] = image
    new_solution_ref[...] = solution


def forward_kernel(meta_ref, in_ref, scalars_ref, footprint_ref, out_ref, sums_ref):
    blocks = footprint_ref.shape[0]
    rows, soundings, _ = sums_ref.shape
    sums_ref[...] = jnp.zeros_like(sums_ref)

    def product(block):
        row = meta_ref[blocks + block]
        place = meta_ref[2 * blocks + block]
        left = jnp.broadcast_to(in_ref[pl.ds(place, 1), :], (2 * SUB, LANES))
        right = jnp.broadcast_to(in_ref[pl.ds(place + 1, 1), :], (2 * SUB, LANES))
        for start in range(0, soundings, 2 * SUB):
            part = footprint_ref[block, start : start + 2 * SUB, :]
            sums_ref[row, start : start + 2 * SUB, :] += part[:, :LANES] * left + part[:, LANES:] * right

    each(0, blocks, 8, product)
    lanes = lane_ids((8, LANES))
    per_half = LANES // rows
    halves = []
    for half in range(soundings // 8 // per_half):
        packed = [jnp.zeros((8, LANES), F32) for _ in range(4)]
        for at in range(per_half):
            group = half * per_half + at
            for row in range(rows):
                summed = jnp.sum(sums_ref[row, 8 * group : 8 * group + 8, :], axis=1, keepdims=True)
                packed[row % 4] = jnp.where(lanes == rows * at + row, summed, packed[row % 4])
        halves.append((packed[0] + packed[1]) + (packed[2] + packed[3]))
    halves.append(scalars_ref[...])
    out_ref[...] = jnp.concatenate(halves, axis=0)


def adjoint_kernel(iteration, last, *refs):
    meta_ref, own_ref, next_ref, previous_ref, opposite_ref, weights_ref, footprint_ref, *refs = refs
    if iteration > 0:
        state_ref, old_ref, *refs = refs
    if iteration > 1:
        older_ref, *refs = refs
    out_ref, *refs = refs
    blocks = footprint_ref.shape[0]
    peers = out_ref.shape[0] // DELIVER
    summed = (own_ref[...] + opposite_ref[...]) + (next_ref[...] + previous_ref[...])
    forward = jnp.concatenate([summed[0:8], summed[8:16]], axis=1)
    field = weights_ref[...] * forward
    *refs, field_ref = refs
    out_ref[...] = jnp.zeros_like(out_ref)
    spread(field, field_ref)
    def product(block):
        transposed_product(
            footprint_ref, field_ref, out_ref, block, meta_ref[blocks + block], meta_ref[block]
        )

    together = 8
    each(0, blocks - together, together, product)
    sums = [lane_sums(field * forward)]
    if iteration > 0:
        direction = old_ref[...]
        if iteration > 1:
            direction = direction + spanning(state_ref[24:32, :], direction.shape) * older_ref[...]
        sums.append(lane_sums(field * direction))
    if not last:
        refs[0][...] = forward
        if iteration > 0:
            refs[1][...] = direction
    scalars = jnp.sum(summed[16:24] + in_lanes(sums, 3), axis=0, keepdims=True)
    out_ref[pl.ds(FETCH, peers, stride=DELIVER), :] = jnp.broadcast_to(scalars, (peers, LANES))
    for block in range(blocks - together, blocks):
        product(block)


def call(kernel, out_shape, kinds, out_kinds=None, scratch=()):
    spaces = {"v": pltpu.VMEM, "s": pltpu.SMEM, "h": pl.ANY}
    out_kinds = out_kinds or "v" * len(out_shape)
    return pl.pallas_call(
        kernel,
        out_shape=out_shape,
        in_specs=[pl.BlockSpec(memory_space=spaces[kind]) for kind in kinds],
        out_specs=[pl.BlockSpec(memory_space=spaces[kind]) for kind in out_kinds],
        scratch_shapes=list(scratch),
        compiler_params=pltpu.CompilerParams(vmem_limit_bytes=16 * 1024 * 1024),
    )


def per_device(observed, weights, precision_prior, footprint, block_rows, block_cells):
    rows, soundings = observed.shape
    own, width = precision_prior.shape
    cells = CORES * own
    blocks = footprint.shape[0]
    orbits = lax.axis_size("orb")
    reps = lax.axis_size("rep")
    peers = orbits // CORES
    shape = jax.ShapeDtypeStruct
    fetched = shape((peers * FETCH, LANES), F32)
    delivered = shape((peers * DELIVER, LANES), F32)
    packed_shape = shape((8, soundings * rows // 8), F32)
    scalar_shape = shape((8, LANES), F32)
    state_shape = shape((32, LANES), F32)
    region = shape((cells, width), F32)
    field = pltpu.VMEM((rows, soundings, LANES), F32)
    same_core = [[CORES * peer + core for peer in range(peers)] for core in range(CORES)]
    swapped = [(device, device ^ 1) for device in range(orbits)]

    def exchange(array):
        flat = array.reshape(peers, 1, array.shape[0] // peers * LANES)
        flat = lax.all_to_all(
            flat, "orb", split_axis=0, concat_axis=0, axis_index_groups=same_core, tiled=True
        )
        return flat.reshape(array.shape)

    def swap(array):
        return lax.ppermute(array, "orb", swapped)

    in_hbm = [
        pltpu.with_memory_space_constraint(array, pltpu.HBM)
        for array in (block_rows, block_cells, observed, weights, precision_prior, footprint)
    ]
    outgoing, meta, packed_weights, own_prior, footprint = call(
        functools.partial(start_kernel, cells),
        [
            delivered,
            pltpu.SMEM((3 * blocks,), jnp.int32),
            packed_shape,
            pltpu.VMEM(precision_prior.shape, F32),
            pltpu.VMEM(footprint.shape, F32),
        ],
        "hhhhhh",
        "vsvvv",
        [
            pltpu.VMEM(footprint.shape, footprint.dtype),
            field,
            pltpu.SMEM((peers,), jnp.int32),
            pltpu.SMEM((blocks,), jnp.int32),
            pltpu.SMEM((blocks,), jnp.int32),
            pltpu.VMEM(observed.shape, F32),
            pltpu.VMEM(weights.shape, F32),
            pltpu.SemaphoreType.DMA((5,)),
            pltpu.SemaphoreType.DMA((12,)),
        ],
    )(*in_hbm)
    half, collect, pick = call(
        first_gather_kernel,
        [
            shape((cells + own, width), F32),
            shape((cells, 3 * CAP * peers), BF16),
            shape((CAP * peers, 4 * cells), BF16),
        ],
        "vv",
    )(exchange(outgoing), own_prior)
    prior, residual, sums, outgoing = call(
        first_update_kernel, [region, region, scalar_shape, fetched], "vvv"
    )(half, swap(half), pick)
    state, history, images = None, (), ()
    for iteration in range(ITERS):
        first, last = iteration == 0, iteration == ITERS - 1
        (partial,) = call(
            forward_kernel, [shape((24, LANES), F32)], "svvv", scratch=[field]
        )(meta, exchange(outgoing), sums, footprint)
        others = [
            lax.ppermute(partial, "rep", [(device, device ^ by) for device in range(reps)])
            for by in (1, 3, 2)
        ]
        operands = [meta, partial, *others, packed_weights, footprint]
        operands += [] if first else [state, *images]
        outgoing, *images = call(
            functools.partial(adjoint_kernel, iteration, last),
            [delivered] + ([] if last else [packed_shape] * (1 if first else 2)),
            "s" + "v" * (len(operands) - 1),
            scratch=[field],
        )(*operands)
        (half,) = call(gather_kernel, [shape((cells + 8, width), F32)], "vv")(
            exchange(outgoing), collect
        )
        operands = [half, swap(half), pick, prior, residual]
        operands += [] if first else [state, *history]
        results = call(
            functools.partial(update_kernel, first, last),
            [shape((own, width), F32)] * 2
            if last
            else [region, scalar_shape, fetched, state_shape, region, region, region],
            "v" * len(operands),
        )(*operands)
        if not last:
            residual, sums, outgoing, state, *history = results
    return tuple(results)


def solution(mesh):
    in_specs = (
        P("orb", None),
        P("orb", None),
        P("orb", "rep"),
        P("orb", None, "rep"),
        P("orb"),
        P("orb"),
    )
    out_specs = (P("orb", "rep"), P("orb", "rep"))
    return jax.shard_map(
        per_device, mesh=mesh, in_specs=in_specs, out_specs=out_specs, check_vma=False
    )
```
